32 devices in a mesh: row: 8 (over z, x), col: 4 (over y, core).
Axes of the slice: x: 2, y: 2, z: 4, core: 2. Of those that a mesh axis runs over, the one named last changes fastest.
Arguments:
- rhs: float32 [2048, 512], P('row', 'col'), may hold values from -6 to 6
- factor: float32 [2048, 4, 256], P('row', None, 'col'), may hold values from -0.1875 to 0.1875
- inverses: float32 [4, 256, 256], P(None, 'row'), may hold values from -2 to 2, as said below
Outputs:
- solved: float32 [2048, 512], P('row', 'col')
The draws below stay inside these ranges and needn't reach their ends.
Inputs may be any that keep to these rules, and one draw needn't show every extreme that they name: Each inverses[k] is lower triangular with diagonal entries between 0.5 and 2.
All inputs are finite; a program needn't handle non-finite values.
Results may differ from the reference program's by a relative error of at most 0.0001.
Values sent between devices are 32-bit elements; how exact they have to be, the bound alone decides.
No kernel may reach another device: no remote copies, remote signals or barrier semaphores. Data moves between devices by JAX's collectives and lax.ppermute only.
A program may use at most 64 MiB of HBM per device.

```python
import math
import jax
import jax.numpy as jnp
from jax import lax

P_SIZE = 256
NPAN = 4
NC = 512
ROWS = 2048
N_ROW = 8


def draw_inverses(key, part):
    key_scale, key_spread = jax.random.split(key)
    row_ids = lax.broadcasted_iota(jnp.int32, (NPAN, P_SIZE, P_SIZE), 1)
    col_ids = lax.broadcasted_iota(jnp.int32, (NPAN, P_SIZE, P_SIZE), 2)
    lower = (row_ids > col_ids).astype(jnp.float32)
    diagonal_mask = (row_ids == col_ids).astype(jnp.float32)
    scales = jnp.exp(jax.random.uniform(key_scale, (NPAN, P_SIZE, 1), minval=math.log(0.5), maxval=math.log(2.0)))
    spread = jnp.clip(jax.random.normal(key_spread, (NPAN, P_SIZE, P_SIZE)), -4.0, 4.0) * (0.6 / math.sqrt(P_SIZE))
    return diagonal_mask * scales + lower * spread


def steps_of(own_key, dims, cuts, low, largest):
    def one(axis_at, parts):
        draws = jax.random.uniform(jax.random.fold_in(jax.random.fold_in(own_key, 6), axis_at), (parts,), jnp.float32, low / len(cuts), largest / len(cuts))
        return jnp.repeat(jnp.exp(draws), dims[axis_at] // parts).reshape((-1,) + (1,) * (len(dims) - axis_at - 1))

    loudness = one(*cuts[0])
    for cut in cuts[1:]:
        loudness = loudness * one(*cut)
    return loudness


def centred(own_key, extent, deviation, reach, shards=(), held_as=jnp.bfloat16):
    entries = deviation * jax.random.normal(own_key, extent, jnp.float32)
    if shards:
        entries = entries * steps_of(own_key, extent, shards, -0.22, 0.18)
    return jnp.clip(entries, -reach, reach).astype(held_as)


def setup_inputs(seed: int = 0) -> dict:
    splits = jax.random.split(jax.random.key(seed), 4)
    rhs = centred(splits[0], (ROWS, NC), 1.0, 6.0, ((0, 8), (1, 4)), jnp.float32)
    factor = centred(splits[1], (ROWS, NPAN, P_SIZE), (NPAN * P_SIZE) ** -0.5, 0.1875, ((0, 8), (2, 4)), jnp.float32)
    inverses = draw_inverses(jax.random.fold_in(splits[3], 71), 0)
    return {"rhs": rhs, "factor": factor, "inverses": inverses}


def reference(rhs, factor, inverses):
    blocks = rhs.reshape(N_ROW, P_SIZE, NC)
    panels = factor.reshape(N_ROW, P_SIZE, NPAN, P_SIZE)
    running = jnp.zeros_like(blocks)
    order = jnp.arange(N_ROW, dtype=jnp.int32)
    solved = blocks
    for section in range(NPAN):
        solution_block = jnp.dot(inverses[section], blocks[section] - running[section], precision=lax.Precision.HIGHEST, preferred_element_type=jnp.float32)
        weight = (order > section).astype(jnp.float32)
        update = jnp.einsum("bij,jc->bic", panels[:, :, section, :], solution_block, precision=lax.Precision.HIGHEST)
        running = running + weight[:, None, None] * update
        solved = solved.at[section].set(solution_block)
    later = blocks - running
    final = jnp.where((order >= NPAN)[:, None, None], later, solved)
    return final.reshape(ROWS, NC)
```

```python
import jax
import jax.numpy as jnp
from jax import lax
from jax.sharding import PartitionSpec as P

AXES = ("row", "col")


def dot(left, right):
    return jnp.dot(left, right, precision=lax.Precision.HIGHEST, preferred_element_type=jnp.float32)


def solution(mesh):
    n_row, n_col = mesh.shape["row"], mesh.shape["col"]
    n_pair, n_half = n_row // 2, n_col // 2

    def hop(value, move):
        edges = []
        for q in range(n_pair):
            for x in range(2):
                for j in range(n_half):
                    for k in range(2):
                        end = move(q, x, j, k)
                        if end is not None:
                            a, b, c, d = end
                            edges.append(((q * 2 + x) * n_col + j * 2 + k, (a * 2 + b) * n_col + c * 2 + d))
        return lax.ppermute(value, AXES, edges)

    def body(rhs, factor, inverses):
        n_pan = factor.shape[1]
        n_win = n_pan // 2
        rows, part = factor.shape[0], factor.shape[2]
        shard = inverses.shape[1]
        row, col = lax.axis_index("row"), lax.axis_index("col")
        q, x, j, k = row // 2, row % 2, col // 2, col % 2
        flat = jnp.transpose(factor, (1, 0, 2))
        own = [flat] + [hop(flat, lambda q, x, j, k, s=s: (q, x, (j + s) % n_half, k)) for s in range(1, n_half)]
        own = jnp.stack(own)
        beside = hop(own, lambda q, x, j, k: (q, 1 - x, j, k))
        mine = jnp.where(x == k, own, beside)
        other = hop(jnp.where(x == k, beside, own), lambda q, x, j, k: (q, x, j, 1 - k))
        pieces = jnp.concatenate([mine, other])
        block = [jnp.concatenate([pieces[i, p] for i in range(n_col)], axis=1) for p in range(n_pan)]
        order = [((j - s) % n_half) * 2 + c for c in (k, 1 - k) for s in range(n_half)]

        def ordered(solved):
            return jnp.concatenate([lax.dynamic_slice_in_dim(solved, part * o, part) for o in order])

        def panels_for(target):
            return lax.dynamic_slice_in_dim(inverses, jnp.clip(2 * target, 0, n_pan - 2), 2)

        parts = []
        turned = lambda q, x, j, k: (q, k, j, x)
        for s in range(n_pair):
            sent = panels_for((q - s) % n_pair)

            def move(q, x, j, k, s=s):
                t = (q - s) % n_pair
                return (t, k, j, x) if t < n_win else None

            parts.append(hop(sent, move))
        got = jnp.stack(parts)
        got = jnp.roll(got, q, axis=0) if False else got
        keep = jnp.where(k == 0, got[:, 0], got[:, 1])
        send = jnp.where(k == 0, got[:, 1], got[:, 0])
        recv = hop(send, lambda q, x, j, k: (q, x, j, 1 - k) if q < n_win else None)
        even = jnp.where(k == 0, keep, recv)
        odd = jnp.where(k == 0, recv, keep)
        inverse = jnp.stack([even, odd], axis=1).reshape(n_row * shard, -1)
        inverse = jnp.roll(inverse, q * 2 * shard, axis=0)
        rhs_w = hop(rhs, turned)
        base = dot(inverse, rhs_w)
        steps = [dot(inverse, block[p]) for p in range(n_pan - 1)]

        known = []
        result = jnp.zeros_like(rhs)
        for w in range(n_win):
            first = base - sum(dot(steps[p], ordered(known[p])) for p in range(2 * w)) if w else base
            got_first = hop(first, lambda q, x, j, k: (q, x, j, 1 - k) if q == w else None)
            second = base - sum(
                dot(steps[p], ordered(v)) for p, v in enumerate(known + [got_first])
            )
            solved = jnp.where(k == 0, first, second)
            result = jnp.where(q == w, solved, result)
            arrived = jnp.zeros_like(rhs)
            for t in range(w + 1, n_pair):
                arrived = arrived + hop(solved, lambda q, x, j, k: (t, x, j, k) if q == w else None)
            swapped = hop(arrived, lambda q, x, j, k: (q, x, j, 1 - k) if q > w else None)
            known = known + [jnp.where(k == 0, arrived, swapped), jnp.where(k == 0, swapped, arrived)]
        final = rhs_w - sum(dot(block[p], ordered(known[p])) for p in range(n_pan))
        result = jnp.where(q < n_win, result, final)
        return hop(result, turned)

    placed = (P("row", "col"), P("row", None, "col"), P(None, "row", None))
    return jax.shard_map(body, mesh=mesh, in_specs=placed, out_specs=P("row", "col"), check_vma=False)
```

```python
import jax
import jax.numpy as jnp
from jax import lax
from jax.sharding import PartitionSpec as P

AXES = ("row", "col")


def dot(left, right):
    return jnp.dot(left, right, precision=lax.Precision.HIGHEST, preferred_element_type=jnp.float32)


def after(value, earlier):
    return lax.optimization_barrier((value, earlier))[0]


def solution(mesh):
    n_row, n_col = mesh.shape["row"], mesh.shape["col"]
    n_pair, n_half = n_row // 2, n_col // 2

    def hop(value, move):
        edges = []
        for q in range(n_pair):
            for x in range(2):
                for j in range(n_half):
                    for k in range(2):
                        end = move(q, x, j, k)
                        if end is not None:
                            a, b, c, d = end
                            edges.append(((q * 2 + x) * n_col + j * 2 + k, (a * 2 + b) * n_col + c * 2 + d))
        return lax.ppermute(value, AXES, edges)

    def body(rhs, factor, inverses):
        rows, n_pan, part = factor.shape
        width = rhs.shape[1]
        shard, wide = inverses.shape[1:]
        n_win = n_pan // 2
        row, col = lax.axis_index("row"), lax.axis_index("col")
        q, x, j, k = row // 2, row % 2, col // 2, col % 2

        def along(value, which):
            shifted = [
                hop(value, lambda q, x, j, k, s=s: (q, x, (j + s) % n_half, k) if which(q) else None)
                for s in range(1, n_half)
            ]
            return jnp.stack([value] + shifted)

        def swap_rows(value, which):
            return hop(value, lambda q, x, j, k: (q, 1 - x, j, k) if which(q) else None)

        def swap_cores(value, which):
            return hop(value, lambda q, x, j, k: (q, x, j, 1 - k) if which(q) else None)

        def panels_for(target):
            return lax.dynamic_slice_in_dim(inverses, jnp.clip(2 * target, 0, n_pan - 2), 2)

        across = jnp.transpose(factor, (1, 2, 0))
        head_own = along(across[0], lambda q: q == 0)

        parts = []
        for s in range(n_pair - 1, 0, -1):

            def inward(q, x, j, k, s=s):
                t = (q - s) % n_pair
                return (t, k, j, x) if t < n_win else None

            parts.append(hop(panels_for((q - s) % n_pair), inward))
        parts = jnp.stack(parts[::-1])
        half = rows // 2
        here = panels_for(q)
        folded = jnp.concatenate([rhs[:half], rhs[half:]], axis=1).reshape(-1, wide)
        packed = jnp.concatenate([folded, here.reshape(-1, wide)])
        beside = swap_rows(packed, lambda q: q < n_win)
        there = beside[-2 * shard :].reshape(2, shard, wide)
        folded = beside[: -2 * shard].reshape(half, 2 * width)
        rhs_beside = jnp.concatenate([folded[:, :width], folded[:, width:]])
        rhs_even = jnp.where(x == 0, rhs, rhs_beside)
        rhs_odd = jnp.where(x == 0, rhs_beside, rhs)

        whole_own = along(across, lambda q: q > 0)
        head_beside = hop(head_own, lambda q, x, j, k: (q, 0, j, k) if q == 0 and x == 1 else None)
        head_odd = jnp.where(x == 0, head_beside, head_own).reshape(-1, rows)

        crossed = swap_cores(parts, lambda q: q < n_win)
        even_row = jnp.concatenate([jnp.where(x == 0, here, there)[None], jnp.where(k == 0, parts, crossed)])
        odd_row = jnp.concatenate([jnp.where(x == 0, there, here)[None], jnp.where(k == 0, crossed, parts)])
        inverse = jnp.stack([even_row, odd_row], axis=1)
        inverse = jnp.transpose(inverse, (2, 0, 1, 3, 4)).reshape(2, n_row * shard, wide)
        inverse = jnp.roll(inverse, q * 2 * shard, axis=1)

        order = [((j - s) % n_half) * 2 + c for c in (k, 1 - k) for s in range(n_half)]

        def ordered(solved):
            return jnp.concatenate([lax.dynamic_slice_in_dim(solved, part * o, part) for o in order])

        head_full = jnp.concatenate([head_odd, swap_cores(head_odd, lambda q: q == 0)])

        near = n_pan - 1
        tail_beside = swap_rows(whole_own[:, :near], lambda q: 0 < q < n_win)
        whole_other = swap_cores(whole_own, lambda q: q > 0)

        solved = []
        first = dot(inverse[0], rhs_even)
        climb = [hop(first, lambda q, x, j, k: (1, x, j, k) if q == 0 else None)]
        second = dot(inverse[1], rhs_odd - dot(head_full.T, ordered(first)))
        climb.append(hop(second, lambda q, x, j, k: (1, x, j, k) if q == 0 else None))
        solved += [first, second]
        result = jnp.where(x == 0, first, second)

        tail_other = swap_cores(after(tail_beside, climb[1]), lambda q: 0 < q < n_win)
        own_full = [
            jnp.concatenate([whole_own[:, p].reshape(-1, rows), whole_other[:, p].reshape(-1, rows)])
            for p in range(n_pan)
        ]
        beside_full = [
            jnp.concatenate([tail_beside[:, p].reshape(-1, rows), tail_other[:, p].reshape(-1, rows)])
            for p in range(near)
        ]
        even_full = [jnp.where(x == 0, own_full[p], beside_full[p]) for p in range(near)]
        odd_full = [jnp.where(x == 0, beside_full[p], own_full[p]) for p in range(near)]

        known = climb
        for w in range(1, n_win):
            left_even, left_odd = rhs_even, rhs_odd
            for p, v in enumerate(known):
                turned = ordered(v)
                left_even = left_even - dot(even_full[p].T, turned)
                left_odd = left_odd - dot(odd_full[p].T, turned)
            first = dot(inverse[0], left_even)
            second = dot(inverse[1], left_odd - dot(odd_full[2 * w].T, ordered(first)))
            solved += [first, second]
            result = jnp.where(q == w, jnp.where(x == 0, first, second), result)
            if w + 1 < n_win:
                known = [
                    v + hop(v if q_from < w else u, lambda q, x, j, k: (w + 1, x, j, k) if q == w else None)
                    for v, u, q_from in ()
                ]

        depth = n_pair - n_win
        waves = []
        for i in range(near - 1 + depth):
            value = waves[-1] if waves else rhs
            if i < near:
                value = jnp.where(q < n_win, solved[i], value)
            origin = i // 2 if i < near else None

            def move(q, x, j, k):
                if q == origin:
                    return (n_win, x, j, k)
                if n_win <= q < n_pair - 1 and i > q - n_win and i - 1 - (q - n_win) < near:
                    return (q + 1, x, j, k)
                return None

            waves.append(hop(value, move))
        last = 0
        for t in range(n_pair - 1, n_win - 1, -1):
            last = last + hop(solved[-1], lambda q, x, j, k: (t, x, j, k) if q == n_win - 1 else None)
        final = rhs
        for p in range(near):
            value = waves[p]
            for d in range(1, depth):
                value = jnp.where(q == n_win + d, waves[p + d], value)
            final = final - dot(own_full[p].T, ordered(value))
        final = final - dot(own_full[near].T, ordered(last))
        return jnp.where(q < n_win, result, final)

    placed = (P("row", "col"), P("row", None, "col"), P(None, "row", None))
    return jax.shard_map(body, mesh=mesh, in_specs=placed, out_specs=P("row", "col"), check_vma=False)
```

```python
import itertools

import jax
import jax.numpy as jnp
from jax import lax
from jax.experimental import pallas as pl
from jax.experimental.pallas import tpu as pltpu
from jax.sharding import PartitionSpec as P

AXES = ("row", "col")
VMEM = pl.BlockSpec(memory_space=pltpu.VMEM)
ANY = pl.BlockSpec(memory_space=pl.ANY)
FREE = pl.CostEstimate(flops=0, bytes_accessed=0, transcendentals=0)
LIMIT = 24 * 1024 * 1024


def split(value):
    high = value.astype(jnp.bfloat16)
    return high, (value - high.astype(jnp.float32)).astype(jnp.bfloat16)


def dot(left, right, over=1):
    (a, b), (c, d) = split(left), split(right)

    def one(u, v):
        return lax.dot_general(u, v, (((over,), (0,)), ((), ())), preferred_element_type=jnp.float32)

    return one(a, c) + (one(a, d) + one(b, c))


def call(body, shapes, held, first=(), last=(), home=False, scratch=()):
    out = [jax.ShapeDtypeStruct(s, jnp.float32) if home else pltpu.VMEM(s, jnp.float32) for s in shapes]
    n_in, n_last = len(first) + len(held), len(last)

    def kernel(*refs):
        body(*refs[:n_in], *refs[n_in + n_last :])

    got = pl.pallas_call(
        kernel,
        out_shape=out,
        in_specs=[ANY] * len(first) + [VMEM] * len(held) + [ANY] * n_last,
        out_specs=[VMEM] * len(shapes),
        scratch_shapes=scratch,
        cost_estimate=FREE,
        compiler_params=pltpu.CompilerParams(vmem_limit_bytes=LIMIT),
    )(*[pltpu.with_memory_space_constraint(v, pltpu.HBM) for v in first], *[pltpu.with_memory_space_constraint(v, pltpu.VMEM) for v in held], *last)
    return got[0] if len(shapes) == 1 else got


def solution(mesh):
    n_row, n_col = mesh.shape["row"], mesh.shape["col"]
    n_pair, n_half = n_row // 2, n_col // 2

    def place():
        row, col = lax.axis_index("row"), lax.axis_index("col")
        return row // 2, row % 2, col // 2, col % 2

    def hop(value, move):
        edges = []
        for q in range(n_pair):
            for x in range(2):
                for j in range(n_half):
                    for k in range(2):
                        a, b, c, d = move(q, x, j, k)
                        edges.append(((q * 2 + x) * n_col + j * 2 + k, (a * 2 + b) * n_col + c * 2 + d))
        return lax.ppermute(value, AXES, edges)

    def along(value):
        return [hop(value, lambda q, x, j, k, s=s: (q, x, (j + s) % n_half, k)) for s in range(1, n_half)]

    def swap_rows(value):
        return hop(value, lambda q, x, j, k: (q, 1 - x, j, k))

    def swap_cores(value):
        return hop(value, lambda q, x, j, k: (q, x, j, 1 - k))

    def climb(value, w, t):
        free = [q for q in range(n_pair) if q != w]
        ends = [q for q in range(n_pair) if q != t]
        if n_pair <= 6:
            choices = itertools.permutations(ends)
        else:
            choices = (ends[r:] + ends[:r] for r in range(len(ends)))
        choices = [c for c in choices if all(a != b for a, b in zip(free, c, strict=True))]
        best = min(choices, key=lambda c: sum(max(b - a, 0) for a, b in zip(free, c, strict=True)))
        to = dict(zip(free, best, strict=True)) | {w: t}
        return hop(value, lambda q, x, j, k: (to[q], x, j, k))

    def body(rhs, factor, inverses):
        rows, n_pan, part = factor.shape
        width = rhs.shape[1]
        shard, wide = inverses.shape[1:]
        n_win, near = n_pan // 2, n_pan - 1
        half, units, pair = rows // 2, near * part, 2 * shard
        at_head = half + pair
        at_parts = (n_pair - 1) * pair

        def unfold(ref):
            return jnp.concatenate([ref[:half, :width], ref[:half, width:]])

        def arrived(values):
            got = values[0]
            for i, value in enumerate(values[1:], 1):
                got = jnp.where(place()[0] == n_pair - 1 - i, value, got)
            return got

        def ordered(refs, at=0):
            q, x, j, k = place()
            got = []
            for c in (k, 1 - k):
                for s in range(n_half):
                    start = pl.multiple_of((lax.rem(j - s + n_half, n_half) * 2 + c) * part + at, part)
                    got.append(arrived([ref[pl.ds(start, part), :] for ref in refs]))
            return jnp.concatenate(got)

        def turn(value):
            q, step = place()[0], 1
            while step < n_pair:
                run = step * pair
                pieces = [value[at : at + run] for at in range(0, n_pair * pair, run)]
                other = [pieces[i ^ 1] for i in range(len(pieces))]
                value = jnp.where((q // step) % 2 == 1, jnp.concatenate(other), value)
                step *= 2
            return value

        across = jnp.transpose(factor, (1, 2, 0)).reshape(-1, rows)

        def prepare(rhs, across, inverses, packed, own, here, mine, *refs):
            sent, panels, sems = refs[:-2], refs[-2], refs[-1]
            q = place()[0]
            copies = [
                pltpu.make_async_copy(a, b, sems.at[i])
                for i, (a, b) in enumerate(((rhs, here), (inverses, panels), (across, own)))
            ]
            for copy in copies:
                copy.start()
            copies[0].wait()
            packed[:half] = jnp.concatenate([here[:half], here[half:]], axis=1)
            copies[1].wait()

            def both(target):
                first = 2 * jnp.minimum(target, n_win - 1)
                return jnp.concatenate([panels[first], panels[first + 1]])

            for s, ref in enumerate(sent, 1):
                ref[...] = both(jnp.bitwise_xor(q, s))
            mine[...] = both(q)
            packed[half:at_head] = mine[...]
            copies[2].wait()
            packed[at_head:] = own[:part]

        packed, own, rhs, mine, *sent = call(
            prepare,
            [(at_head + part, wide), (n_pan * part, rows), (rows, width)]
            + [(pair, wide)] * n_pair,
            [],
            first=[rhs, across, inverses],
            scratch=[pltpu.VMEM((n_pan, shard, wide), jnp.float32), pltpu.SemaphoreType.DMA((3,))],
        )

        beside = swap_rows(packed)
        parts = [
            hop(sent[s - 1], lambda q, x, j, k, s=s: (q ^ s, k, j, x)) for s in range(1, n_pair)
        ]

        def cut(own, tail):
            tail[...] = own[part:units]

        tail = call(cut, [(units - part, rows)], [own])
        tail_beside = swap_rows(tail)

        def pick_head(own, beside, head):
            head[...] = jnp.where(place()[1] == 0, beside[at_head:], own[:part])

        head = call(pick_head, [(part, rows)], [own, beside])
        head_along = along(head)

        own_along = along(own)

        def join(beside, tail, joined):
            joined[:part] = beside[at_head:]
            joined[part:] = tail[...]

        joined = call(join, [(units, rows)], [beside, tail_beside])
        joined_along = along(joined)

        def pack(*refs):
            packed = refs[-1]
            for s in range(n_pair - 1):
                packed[s * pair : (s + 1) * pair] = refs[s][...]
            for s in range(n_half):
                packed[at_parts + s * part : at_parts + (s + 1) * part] = refs[n_pair - 1 + s][...]

        packed = call(pack, [(at_parts + n_half * part, wide)], [*parts, head, *head_along])
        other = swap_cores(packed)

        def solve_first(packed, other, mine, beside, rhs, solved, inverse):
            q, x, j, k = place()
            theirs = beside[half:at_head]
            for m in range(2):
                at = m * shard
                got = [mine[at : at + shard], theirs[at : at + shard]]
                got = [jnp.where(x == 0, got[0], got[1]), jnp.where(x == 0, got[1], got[0])]
                for s in range(n_pair - 1):
                    a, b = (ref[s * pair + at : s * pair + at + shard] for ref in (packed, other))
                    got += [jnp.where(k == 0, a, b), jnp.where(k == 0, b, a)]
                inverse[m] = jnp.concatenate(got)
            a, b = rhs[...], unfold(beside)
            first = turn(dot(inverse[0], jnp.where(x == 0, a, b)))
            solved[:rows] = first
            panel = jnp.concatenate([packed[at_parts:], other[at_parts:]])
            left = jnp.where(x == 0, b, a) - dot(panel, ordered([solved]), 0)
            second = turn(dot(inverse[1], left))
            solved[rows:] = second

        solved, inverse = call(
            solve_first, [(2 * rows, width), (2, wide, wide)], [packed, other, mine, beside, rhs]
        )

        def choose(solved, either):
            either[...] = jnp.where(place()[1] == 0, solved[:rows], solved[rows:])

        known = [climb(solved, 0, 1)]
        either = call(choose, [(rows, width)], [solved])
        results = [either]

        whole = n_pan * part

        def stack(*refs):
            at = 0
            for ref in refs[:-1]:
                refs[-1][at : at + ref.shape[0]] = ref[...]
                at += ref.shape[0]

        soon = call(stack, [(n_half * whole + units, rows)], [own, *own_along, joined])
        soon = (soon, swap_cores(soon))
        late = call(stack, [((n_half - 1) * units, rows)], joined_along, last=[either])
        late = (late, swap_cores(late))
        blocks = [soon[0], soon[1], late[0], late[1]]

        def columns(blocks, theirs, panel, count=1):
            got = []
            for p in range(panel, panel + count):
                for core in range(2):
                    for s in range(n_half):
                        ref, at = blocks[core], s * whole
                        if theirs:
                            at = n_half * whole
                            if s:
                                ref, at = blocks[2 + core], (s - 1) * units
                        got.append(ref[at + p * part : at + (p + 1) * part])
            return jnp.concatenate(got)

        def lift(value, w):
            return [climb(value, w, t) for t in range(n_pair - 1, n_win - 1, -1)]

        lifted = [lift(either, 0)]
        for w in range(1, n_win):

            def solve_next(inverse, beside, rhs, *refs, w=w):
                blocks, known, (solved, either) = refs[:4], refs[4:-2], refs[-2:]
                x = place()[1]
                turned = [ordered([ref], at) for ref in known for at in (0, rows)]
                lefts = [
                    start - dot(columns(blocks, theirs, 0, 2 * w), jnp.concatenate(turned), 0)
                    for theirs, start in ((False, rhs[...]), (True, unfold(beside)))
                ]
                first = turn(dot(inverse[0], jnp.where(x == 0, lefts[0], lefts[1])))
                solved[:rows] = first
                block = jnp.where(
                    x == 0, columns(blocks, True, 2 * w), columns(blocks, False, 2 * w)
                )
                left = jnp.where(x == 0, lefts[1], lefts[0]) - dot(block, ordered([solved]), 0)
                second = turn(dot(inverse[1], left))
                solved[rows:] = second
                either[...] = jnp.where(x == 0, first, second)

            solved, either = call(
                solve_next,
                [(2 * rows, width), (rows, width)],
                [inverse, beside, rhs, *blocks, *known],
            )
            results.append(either)
            if w + 1 < n_win:
                lifted.append(lift(either, w))
                known = [climb(v, w, w + 1) for v in known + [solved]]
        final = lift(solved, n_win - 1)

        def gather(*refs):
            refs[-1][...] = arrived([ref[...] for ref in refs[:-1]])

        early = []
        for v in lifted:
            v = call(gather, [(rows, width)], v, last=[solved])
            early += [v, swap_rows(v)]

        def update(rhs, *refs):
            blocks, early, out = refs[:4], refs[4:-1], refs[-1]
            x = place()[1]
            turned = []
            for v, t in zip(early[::2], early[1::2], strict=True):
                a, b = ordered([v]), ordered([t])
                turned += [jnp.where(x == 0, a, b), jnp.where(x == 0, b, a)]
            out[...] = rhs[...] - dot(columns(blocks, False, 0, len(turned)), jnp.concatenate(turned), 0)

        left = call(update, [(rows, width)], [rhs, *blocks, *early])

        def finish(left, *refs):
            blocks, results, final, out = refs[:4], refs[4 : 4 + n_win], refs[4 + n_win : -1], refs[-1]
            q = place()[0]
            turned = jnp.concatenate([ordered(final), ordered(final, rows)])
            out[...] = left[...] - dot(columns(blocks, False, n_pan - 2, 2), turned, 0)
            for w in range(n_win):

                @pl.when(q == w)
                def _(w=w):
                    out[...] = results[w][...]

        return call(finish, [(rows, width)], [left, *blocks, *results, *final], home=True)

    placed = (P("row", "col"), P("row", None, "col"), P(None, "row", None))
    return jax.shard_map(body, mesh=mesh, in_specs=placed, out_specs=P("row", "col"), check_vma=False)
```

```python
import functools

import jax
import jax.numpy as jnp
from jax import lax
from jax.experimental import pallas as pl
from jax.experimental.pallas import tpu as pltpu
from jax.sharding import PartitionSpec as P

AXES = ("row", "col")
VMEM = pl.BlockSpec(memory_space=pltpu.VMEM)
ANY = pl.BlockSpec(memory_space=pl.ANY)
FREE = pl.CostEstimate(flops=0, bytes_accessed=0, transcendentals=0)
LIMIT = 24 * 1024 * 1024


def split(value):
    high = value.astype(jnp.bfloat16)
    return high, (value - high.astype(jnp.float32)).astype(jnp.bfloat16)


def dot(left, right, over=(1, 0)):
    (a, b), (c, d) = split(left), split(right)

    def one(u, v):
        return lax.dot_general(u, v, (((over[0],), (over[1],)), ((), ())), preferred_element_type=jnp.float32)

    return one(a, c) + (one(a, d) + one(b, c))


def call(body, shapes, held, first=(), last=(), home=False, scratch=()):
    out = [jax.ShapeDtypeStruct(s, jnp.float32) if home else pltpu.VMEM(s, jnp.float32) for s in shapes]
    n_in, n_last = len(first) + len(held), len(last)

    def kernel(*refs):
        body(*refs[:n_in], *refs[n_in + n_last :])

    got = pl.pallas_call(
        kernel,
        out_shape=out,
        in_specs=[ANY] * len(first) + [VMEM] * len(held) + [ANY] * n_last,
        out_specs=[VMEM] * len(shapes),
        scratch_shapes=scratch,
        cost_estimate=FREE,
        compiler_params=pltpu.CompilerParams(vmem_limit_bytes=LIMIT),
    )(
        *[pltpu.with_memory_space_constraint(v, pltpu.HBM) for v in first],
        *[pltpu.with_memory_space_constraint(v, pltpu.VMEM) for v in held],
        *last,
    )
    return got[0] if len(shapes) == 1 else got


def solution(mesh):
    n_row, n_col = mesh.shape["row"], mesh.shape["col"]
    n_pair, n_half = n_row // 2, n_col // 2

    def place():
        row, col = lax.axis_index("row"), lax.axis_index("col")
        return row // 2, row % 2, col // 2, col % 2

    def hop(value, move):
        edges = []
        for q in range(n_pair):
            for x in range(2):
                for j in range(n_half):
                    for k in range(2):
                        a, b, c, d = move(q, x, j, k) or (q, x, j, 1 - k)
                        edges.append(((q * 2 + x) * n_col + j * 2 + k, (a * 2 + b) * n_col + c * 2 + d))
        return lax.ppermute(value, AXES, edges)

    def every(q):
        return True

    def along(value, which=every):
        return [
            hop(value, lambda q, x, j, k, s=s: (q, x, (j + s) % n_half, k) if which(q) else None)
            for s in range(1, n_half)
        ]

    def swap_rows(value, which=every):
        return hop(value, lambda q, x, j, k: (q, 1 - x, j, k) if which(q) else None)

    def swap_cores(value):
        return hop(value, lambda q, x, j, k: None)

    def climb(value, w, t):
        return hop(value, lambda q, x, j, k: ({w: t, t: w}[q], x, j, k) if q in (w, t) else None)

    def body(rhs, factor, inverses):
        rows, n_pan, part = factor.shape
        width = rhs.shape[1]
        shard, wide = inverses.shape[1:]
        n_win = n_pan // 2
        half, pair, whole = rows // 2, 2 * shard, n_pan * part
        units = (n_pan - 2) * part
        at_own = (n_pair - 1) * pair
        at_beside = at_own + n_half * whole

        def unfold(ref):
            return jnp.concatenate([ref[:half, :width], ref[:half, width:]])

        def ordered(ref):
            q, x, j, k = place()
            got = []
            for c in (k, 1 - k):
                for s in range(n_half):
                    start = pl.multiple_of((lax.rem(j - s + n_half, n_half) * 2 + c) * part, part)
                    got.append(ref[pl.ds(start, part), :])
            return jnp.concatenate(got)

        def turn(value):
            q, step = place()[0], 1
            while step < n_pair:
                run = step * pair
                pieces = [value[at : at + run] for at in range(0, n_pair * pair, run)]
                other = [pieces[i ^ 1] for i in range(len(pieces))]
                value = jnp.where((q // step) % 2 == 1, jnp.concatenate(other), value)
                step *= 2
            return value

        across = jnp.transpose(factor, (1, 2, 0)).reshape(-1, rows)

        def prepare(rhs, across, inverses, packed, near, own, here, mine, *refs):
            sent, panels, sems = refs[:-2], refs[-2], refs[-1]
            q = place()[0]
            copies = [
                pltpu.make_async_copy(a, b, sems.at[i])
                for i, (a, b) in enumerate(((rhs, here), (inverses, panels), (across, own)))
            ]
            for copy in copies:
                copy.start()
            copies[0].wait()
            packed[:half] = jnp.concatenate([here[:half], here[half:]], axis=1)
            copies[1].wait()

            def both(target):
                first = 2 * jnp.minimum(target, n_win - 1)
                return jnp.concatenate([panels[first], panels[first + 1]])

            for s, ref in enumerate(sent, 1):
                ref[...] = both(jnp.bitwise_xor(q, s))
            mine[...] = both(q)
            packed[half:] = mine[...]
            copies[2].wait()
            near[...] = own[:units]

        packed, near, own, rhs, mine, *sent = call(
            prepare,
            [(half + pair, wide), (units, rows), (whole, rows), (rows, width)] + [(pair, wide)] * n_pair,
            [],
            first=[rhs, across, inverses],
            scratch=[pltpu.VMEM((n_pan, shard, wide), jnp.float32), pltpu.SemaphoreType.DMA((3,))],
        )

        beside = swap_rows(packed, lambda q: q < n_win)
        near = swap_rows(near, lambda q: 0 < q < n_win)
        parts = [hop(sent[s - 1], lambda q, x, j, k, s=s: (q ^ s, k, j, x)) for s in range(1, n_pair)]
        own_along = along(own)

        def stack(*refs):
            at = 0
            for ref in refs[:-1]:
                refs[-1][at : at + ref.shape[0]] = ref[...]
                at += ref.shape[0]

        soon = call(stack, [(at_beside + units, wide)], [*parts, own, *own_along, near], last=[beside])
        soon = [soon, swap_cores(soon)]
        near_along = along(call(stack, [(units, rows)], [near], last=parts), lambda q: 0 < q < n_win)

        def columns(blocks, panel, count, row=0):
            got = []
            for p in range(panel, panel + count):
                for core in range(2):
                    for s in range(n_half):
                        ref, at = blocks[core], at_own + s * whole
                        if row:
                            at = at_beside
                            if s:
                                ref, at = blocks[2 + core], (s - 1) * units
                        got.append(ref[at + p * part : at + (p + 1) * part])
            return jnp.concatenate(got)

        def solve_first(soon, other, mine, beside, rhs, either, inverse, scratch):
            q, x, j, k = place()
            theirs = beside[half:]
            for m in range(2):
                at = m * shard
                got = [mine[at : at + shard], theirs[at : at + shard]]
                got = [jnp.where(x == 0, got[0], got[1]), jnp.where(x == 0, got[1], got[0])]
                for s in range(n_pair - 1):
                    a, b = (ref[s * pair + at : s * pair + at + shard] for ref in (soon, other))
                    got += [jnp.where(k == 0, a, b), jnp.where(k == 0, b, a)]
                inverse[m] = jnp.concatenate(got)
            first = turn(dot(inverse[0], jnp.where(x == 0, rhs[...], unfold(beside))))
            scratch[...] = first
            either[...] = first

            @pl.when(x == 1)
            def _():
                left = rhs[...] - dot(columns([soon, other], 0, 1), ordered(scratch), (0, 0))
                either[...] = turn(dot(inverse[1], left))

        panel = pltpu.VMEM((rows, width), jnp.float32)
        either, inverse = call(
            solve_first, [(rows, width), (2, wide, wide)], [*soon, mine, beside, rhs], scratch=[panel]
        )
        results = [either]

        def arrive(*refs):
            got = refs[0][...]
            for i, ref in enumerate(refs[1:-1], 1):
                got = jnp.where(place()[0] == n_pair - 1 - i, ref[...], got)
            refs[-1][...] = got

        early, blocks = [], None
        for w in range(n_win - 1):
            here = climb(either, w, w + 1)
            there = swap_rows(here, lambda q, w=w: q == w + 1)
            early.append([climb(either, w, t) for t in range(n_pair - 1, w + 1, -1)])
            late = call(stack, [((n_half - 1) * units, rows)], near_along, last=[here])
            blocks = [*soon, late, swap_cores(late)]

            def lean(inverse, beside, rhs, *refs):
                blocks, here, (fixed, slope, kept) = refs[:4], refs[4], refs[5:]
                x = place()[1]

                def solve(m, start, block, other):
                    fixed[...] = turn(dot(inverse[m], start))
                    slope[...] = turn(dot(inverse[m], block, (1, 1) if other else (1, 0)))

                mine = ordered(here)

                @pl.when(x == 0)
                def _():
                    start = rhs[...] - dot(columns(blocks, 0, 1), mine, (0, 0))
                    solve(0, start, columns(blocks, 1, 1), True)

                @pl.when(x == 1)
                def _():
                    start = unfold(beside) - dot(columns(blocks, 1, 1, 1), mine, (0, 0))
                    solve(0, start, columns(blocks, 0, 1, 1), True)
                    start = rhs[...] - dot(columns(blocks, 1, 1), mine, (0, 0))
                    step = columns(blocks, 2, 1)
                    start = start - dot(step, ordered(fixed), (0, 0))
                    kept[...] = slope[...]
                    block = columns(blocks, 0, 1).T - dot(step, ordered(kept), (0, 0))
                    solve(1, start, block, False)

            def solve_next(fixed, slope, there, either):
                either[...] = fixed[...] - dot(slope[...], ordered(there))

            fixed, slope = call(
                lean,
                [(rows, width), (rows, wide)],
                [inverse, beside, rhs, *blocks, here],
                scratch=[pltpu.VMEM((rows, wide), jnp.float32)],
            )
            either = call(solve_next, [(rows, width)], [fixed, slope, there])
            results.append(either)

        final = [climb(either, n_win - 1, t) for t in range(n_pair - 1, n_win - 1, -1)]
        left = rhs
        for i, values in enumerate([*early, final]):
            value = call(arrive, [(rows, width)], values, last=[either] if i < len(early) else [])
            traded = swap_rows(value, lambda q: q >= n_win)

            def update(start, *refs, other, at=2 * i):
                blocks, value, out = refs[:4], refs[4], refs[5]
                a, b = columns(blocks, at, 1), columns(blocks, at + 1, 1)
                block = jnp.where((place()[1] == 0) == other, b, a)
                out[...] = start[...] - dot(block, ordered(value), (0, 0))

            first = functools.partial(update, other=False)
            left = call(first, [(rows, width)], [left, *blocks, value])
            if i < len(early):
                left = call(functools.partial(update, other=True), [(rows, width)], [left, *blocks, traded])

        def finish(*refs):
            update(*refs[:6], refs[-1], other=True)
            for w in range(n_win):

                @pl.when(place()[0] == w)
                def _(w=w):
                    refs[-1][...] = refs[6 + w][...]

        return call(finish, [(rows, width)], [left, *blocks, traded, *results], home=True)

    placed = (P("row", "col"), P("row", None, "col"), P(None, "row", None))
    return jax.shard_map(body, mesh=mesh, in_specs=placed, out_specs=P("row", "col"), check_vma=False)
```

```python
import functools

import jax
import jax.numpy as jnp
from jax import lax
from jax.experimental import pallas as pl
from jax.experimental.pallas import tpu as pltpu
from jax.sharding import PartitionSpec as P

AXES = ("row", "col")
VMEM = pl.BlockSpec(memory_space=pltpu.VMEM)
ANY = pl.BlockSpec(memory_space=pl.ANY)
FREE = pl.CostEstimate(flops=0, bytes_accessed=0, transcendentals=0)
LIMIT = 24 * 1024 * 1024


def split(value):
    high = value.astype(jnp.bfloat16)
    return high, (value - high.astype(jnp.float32)).astype(jnp.bfloat16)


def dot(left, right, over=(1, 0)):
    (a, b), (c, d) = split(left), split(right)

    def one(u, v):
        return lax.dot_general(u, v, (((over[0],), (over[1],)), ((), ())), preferred_element_type=jnp.float32)

    return one(a, c) + (one(a, d) + one(b, c))


def call(body, shapes, held, first=(), last=(), home=False, scratch=()):
    out = [jax.ShapeDtypeStruct(s, jnp.float32) if home else pltpu.VMEM(s, jnp.float32) for s in shapes]
    n_in, n_last = len(first) + len(held), len(last)

    def kernel(*refs):
        body(*refs[:n_in], *refs[n_in + n_last :])

    got = pl.pallas_call(
        kernel,
        out_shape=out,
        in_specs=[ANY] * len(first) + [VMEM] * len(held) + [ANY] * n_last,
        out_specs=[VMEM] * len(shapes),
        scratch_shapes=scratch,
        cost_estimate=FREE,
        compiler_params=pltpu.CompilerParams(vmem_limit_bytes=LIMIT),
    )(
        *[pltpu.with_memory_space_constraint(v, pltpu.HBM) for v in first],
        *[pltpu.with_memory_space_constraint(v, pltpu.VMEM) for v in held],
        *last,
    )
    return got[0] if len(shapes) == 1 else got


def solution(mesh):
    n_row, n_col = mesh.shape["row"], mesh.shape["col"]
    n_pair, n_half = n_row // 2, n_col // 2

    def place():
        row, col = lax.axis_index("row"), lax.axis_index("col")
        return row // 2, row % 2, col // 2, col % 2

    def hop(value, move):
        edges = []
        for q in range(n_pair):
            for x in range(2):
                for j in range(n_half):
                    for k in range(2):
                        a, b, c, d = move(q, x, j, k) or (q, x, j, 1 - k)
                        edges.append(((q * 2 + x) * n_col + j * 2 + k, (a * 2 + b) * n_col + c * 2 + d))
        return lax.ppermute(value, AXES, edges)

    def every(q):
        return True

    def along(value, which=every):
        return [
            hop(value, lambda q, x, j, k, s=s: (q, x, (j + s) % n_half, k) if which(q) else None)
            for s in range(1, n_half)
        ]

    def swap_rows(value, which=every):
        return hop(value, lambda q, x, j, k: (q, 1 - x, j, k) if which(q) else None)

    def swap_cores(value):
        return hop(value, lambda q, x, j, k: None)

    def climb(value, w, t):
        return hop(value, lambda q, x, j, k: ({w: t, t: w}[q], x, j, k) if q in (w, t) else None)

    def body(rhs, factor, inverses):
        rows, n_pan, part = factor.shape
        width = rhs.shape[1]
        shard, wide = inverses.shape[1:]
        n_win = n_pan // 2
        half, pair, whole = rows // 2, 2 * shard, n_pan * part
        units = (n_pan - 2) * part
        at_own = (n_pair - 1) * pair
        at_beside = at_own + n_half * whole

        def unfold(ref):
            return jnp.concatenate([ref[:half, :width], ref[:half, width:]])

        def ordered(ref):
            q, x, j, k = place()
            got = []
            for c in (k, 1 - k):
                for s in range(n_half):
                    start = pl.multiple_of((lax.rem(j - s + n_half, n_half) * 2 + c) * part, part)
                    got.append(ref[pl.ds(start, part), :])
            return jnp.concatenate(got)

        def turn(value):
            q, step = place()[0], 1
            while step < n_pair:
                run = step * pair
                pieces = [value[at : at + run] for at in range(0, n_pair * pair, run)]
                other = [pieces[i ^ 1] for i in range(len(pieces))]
                value = jnp.where((q // step) % 2 == 1, jnp.concatenate(other), value)
                step *= 2
            return value

        across = jnp.transpose(factor, (1, 2, 0)).reshape(-1, rows)

        def prepare(rhs, across, inverses, packed, own, here, mine, *refs):
            sent, panels, sems = refs[:-2], refs[-2], refs[-1]
            q = place()[0]
            copies = [
                pltpu.make_async_copy(a, b, sems.at[i])
                for i, (a, b) in enumerate(((rhs, here), (inverses, panels), (across, own)))
            ]
            for copy in copies:
                copy.start()
            copies[0].wait()
            packed[:half] = jnp.concatenate([here[:half], here[half:]], axis=1)
            copies[1].wait()

            def both(target):
                first = 2 * jnp.minimum(target, n_win - 1)
                return jnp.concatenate([panels[first], panels[first + 1]])

            for s, ref in enumerate(sent, 1):
                ref[...] = both(jnp.bitwise_xor(q, s))
            mine[...] = both(q)
            packed[half : half + pair] = mine[...]
            copies[2].wait()
            packed[half + pair :] = own[:units]

        packed, own, rhs, mine, *sent = call(
            prepare,
            [(half + pair + units, wide), (whole, rows), (rows, width)] + [(pair, wide)] * n_pair,
            [],
            first=[rhs, across, inverses],
            scratch=[pltpu.VMEM((n_pan, shard, wide), jnp.float32), pltpu.SemaphoreType.DMA((3,))],
        )

        beside = swap_rows(packed, lambda q: q < n_win)
        parts = [hop(sent[s - 1], lambda q, x, j, k, s=s: (q ^ s, k, j, x)) for s in range(1, n_pair)]
        own_along = along(own)

        def stack(*refs):
            at = 0
            for ref in refs[:-1]:
                refs[-1][at : at + ref.shape[0]] = ref[...]
                at += ref.shape[0]

        def mix(beside, *refs):
            stack(*refs)
            refs[-1][at_beside:] = beside[half + pair :]

        def cut(beside, near):
            near[...] = beside[half + pair :]

        soon = call(mix, [(at_beside + units, wide)], [beside, *parts, own, *own_along])
        soon = [soon, swap_cores(soon)]
        near_along = along(call(cut, [(units, rows)], [beside], last=parts), lambda q: 0 < q < n_win)

        def columns(blocks, panel, count, row=0):
            got = []
            for p in range(panel, panel + count):
                for core in range(2):
                    for s in range(n_half):
                        ref, at = blocks[core], at_own + s * whole
                        if row:
                            at = at_beside
                            if s:
                                ref, at = blocks[2 + core], (s - 1) * units
                        got.append(ref[at + p * part : at + (p + 1) * part])
            return jnp.concatenate(got)

        def solve_first(soon, other, mine, beside, rhs, either, inverse, scratch):
            q, x, j, k = place()
            theirs = beside[half : half + pair]
            for m in range(2):
                at = m * shard
                got = [mine[at : at + shard], theirs[at : at + shard]]
                got = [jnp.where(x == 0, got[0], got[1]), jnp.where(x == 0, got[1], got[0])]
                for s in range(n_pair - 1):
                    a, b = (ref[s * pair + at : s * pair + at + shard] for ref in (soon, other))
                    got += [jnp.where(k == 0, a, b), jnp.where(k == 0, b, a)]
                inverse[m] = jnp.concatenate(got)
            first = turn(dot(inverse[0], jnp.where(x == 0, rhs[...], unfold(beside))))
            scratch[...] = first
            either[...] = first

            @pl.when(x == 1)
            def _():
                left = rhs[...] - dot(columns([soon, other], 0, 1), ordered(scratch), (0, 0))
                either[...] = turn(dot(inverse[1], left))

        panel = pltpu.VMEM((rows, width), jnp.float32)
        either, inverse = call(
            solve_first, [(rows, width), (2, wide, wide)], [*soon, mine, beside, rhs], scratch=[panel]
        )
        results = [either]

        def arrive(*refs):
            got = refs[0][...]
            for i, ref in enumerate(refs[1:-1], 1):
                got = jnp.where(place()[0] == n_pair - 1 - i, ref[...], got)
            refs[-1][...] = got

        early, blocks = [], None
        for w in range(n_win - 1):
            here = climb(either, w, w + 1)
            there = swap_rows(here, lambda q, w=w: q == w + 1)
            early.append([climb(either, w, t) for t in range(n_pair - 1, w + 1, -1)])
            late = call(stack, [((n_half - 1) * units, rows)], near_along, last=[here])
            blocks = [*soon, late, swap_cores(late)]

            def lean(inverse, beside, rhs, *refs):
                blocks, here, (fixed, slope, kept) = refs[:4], refs[4], refs[5:]
                x = place()[1]

                def solve(m, start, block, other):
                    fixed[...] = turn(dot(inverse[m], start))
                    slope[...] = turn(dot(inverse[m], block, (1, 1) if other else (1, 0)))

                mine = ordered(here)

                @pl.when(x == 0)
                def _():
                    start = rhs[...] - dot(columns(blocks, 0, 1), mine, (0, 0))
                    solve(0, start, columns(blocks, 1, 1), True)

                @pl.when(x == 1)
                def _():
                    start = unfold(beside) - dot(columns(blocks, 1, 1, 1), mine, (0, 0))
                    solve(0, start, columns(blocks, 0, 1, 1), True)
                    start = rhs[...] - dot(columns(blocks, 1, 1), mine, (0, 0))
                    step = columns(blocks, 2, 1)
                    start = start - dot(step, ordered(fixed), (0, 0))
                    kept[...] = slope[...]
                    block = columns(blocks, 0, 1).T - dot(step, ordered(kept), (0, 0))
                    solve(1, start, block, False)

            def solve_next(fixed, slope, there, either):
                either[...] = fixed[...] - dot(slope[...], ordered(there))

            fixed, slope = call(
                lean,
                [(rows, width), (rows, wide)],
                [inverse, beside, rhs, *blocks, here],
                scratch=[pltpu.VMEM((rows, wide), jnp.float32)],
            )
            either = call(solve_next, [(rows, width)], [fixed, slope, there])
            results.append(either)

        final = [climb(either, n_win - 1, t) for t in range(n_win, n_pair)][::-1]
        left = rhs
        for i, values in enumerate([*early, final]):
            value = call(arrive, [(rows, width)], values, last=[either] if i < len(early) else [])
            traded = swap_rows(value, lambda q: q >= n_win)

            def update(start, *refs, other, at=2 * i):
                blocks, value, out = refs[:4], refs[4], refs[5]
                a, b = columns(blocks, at, 1), columns(blocks, at + 1, 1)
                block = jnp.where((place()[1] == 0) == other, b, a)
                out[...] = start[...] - dot(block, ordered(value), (0, 0))

            first = functools.partial(update, other=False)
            left = call(first, [(rows, width)], [left, *blocks, value])
            if i < len(early):
                left = call(functools.partial(update, other=True), [(rows, width)], [left, *blocks, traded])

        def finish(*refs):
            update(*refs[:6], refs[-1], other=True)
            for w in range(n_win):

                @pl.when(place()[0] == w)
                def _(w=w):
                    refs[-1][...] = refs[6 + w][...]

        return call(finish, [(rows, width)], [left, *blocks, traded, *results], home=True)

    placed = (P("row", "col"), P("row", None, "col"), P(None, "row", None))
    return jax.shard_map(body, mesh=mesh, in_specs=placed, out_specs=P("row", "col"), check_vma=False)
```

```python
import functools

import jax
import jax.numpy as jnp
from jax import lax
from jax.experimental import pallas as pl
from jax.experimental.pallas import tpu as pltpu
from jax.sharding import PartitionSpec as P

AXES = ("row", "col")
VMEM = pl.BlockSpec(memory_space=pltpu.VMEM)
ANY = pl.BlockSpec(memory_space=pl.ANY)
FREE = pl.CostEstimate(flops=0, bytes_accessed=0, transcendentals=0)
LIMIT = 24 * 1024 * 1024


def split(value):
    high = value.astype(jnp.bfloat16)
    return high, (value - high.astype(jnp.float32)).astype(jnp.bfloat16)


def dot(left, right, over=(1, 0)):
    (a, b), (c, d) = split(left), split(right)

    def one(u, v):
        return lax.dot_general(u, v, (((over[0],), (over[1],)), ((), ())), preferred_element_type=jnp.float32)

    return one(a, c) + (one(a, d) + one(b, c))


def call(body, shapes, held, first=(), last=(), home=False, scratch=()):
    out = [jax.ShapeDtypeStruct(s, jnp.float32) if home else pltpu.VMEM(s, jnp.float32) for s in shapes]
    n_in, n_last = len(first) + len(held), len(last)

    def kernel(*refs):
        body(*refs[:n_in], *refs[n_in + n_last :])

    got = pl.pallas_call(
        kernel,
        out_shape=out,
        in_specs=[ANY] * len(first) + [VMEM] * len(held) + [ANY] * n_last,
        out_specs=[VMEM] * len(shapes),
        scratch_shapes=scratch,
        cost_estimate=FREE,
        compiler_params=pltpu.CompilerParams(vmem_limit_bytes=LIMIT),
    )(
        *[pltpu.with_memory_space_constraint(v, pltpu.HBM) for v in first],
        *[pltpu.with_memory_space_constraint(v, pltpu.VMEM) for v in held],
        *last,
    )
    return got[0] if len(shapes) == 1 else got


def solution(mesh):
    n_row, n_col = mesh.shape["row"], mesh.shape["col"]
    n_pair, n_half = n_row // 2, n_col // 2

    def place():
        row, col = lax.axis_index("row"), lax.axis_index("col")
        return row // 2, row % 2, col // 2, col % 2

    def hop(value, move):
        edges = []
        for q in range(n_pair):
            for x in range(2):
                for j in range(n_half):
                    for k in range(2):
                        a, b, c, d = move(q, x, j, k) or (q, x, j, 1 - k)
                        edges.append(((q * 2 + x) * n_col + j * 2 + k, (a * 2 + b) * n_col + c * 2 + d))
        return lax.ppermute(value, AXES, edges)

    def every(q):
        return True

    def along(value, which=every):
        return [
            hop(value, lambda q, x, j, k, s=s: (q, x, (j + s) % n_half, k) if which(q) else None)
            for s in range(1, n_half)
        ]

    def swap_rows(value, which=every):
        return hop(value, lambda q, x, j, k: (q, 1 - x, j, k) if which(q) else None)

    def swap_cores(value):
        return hop(value, lambda q, x, j, k: None)

    def climb(value, w, t):
        return hop(value, lambda q, x, j, k: ({w: t, t: w}[q], x, j, k) if q in (w, t) else None)

    def body(rhs, factor, inverses):
        rows, n_pan, part = factor.shape
        width = rhs.shape[1]
        shard, wide = inverses.shape[1:]
        n_win = n_pan // 2
        half, pair, whole = rows // 2, 2 * shard, n_pan * part
        units = (n_pan - 2) * part
        at_own = (n_pair - 1) * pair
        far = whole - part

        def unfold(ref):
            return jnp.concatenate([ref[:half, :width], ref[:half, width:]])

        def ordered(ref):
            q, x, j, k = place()
            got = []
            for c in (k, 1 - k):
                for s in range(n_half):
                    start = pl.multiple_of((lax.rem(j - s + n_half, n_half) * 2 + c) * part, part)
                    got.append(ref[pl.ds(start, part), :])
            return jnp.concatenate(got)

        def turn(value):
            q, step = place()[0], 1
            while step < n_pair:
                run = step * pair
                pieces = [value[at : at + run] for at in range(0, n_pair * pair, run)]
                other = [pieces[i ^ 1] for i in range(len(pieces))]
                value = jnp.where((q // step) % 2 == 1, jnp.concatenate(other), value)
                step *= 2
            return value

        across = jnp.transpose(factor, (1, 2, 0)).reshape(-1, rows)

        def prepare(rhs, across, inverses, packed, own, here, mine, *refs):
            sent, panels, sems = refs[:-2], refs[-2], refs[-1]
            q = place()[0]
            copies = [
                pltpu.make_async_copy(a, b, sems.at[i])
                for i, (a, b) in enumerate(((rhs, here), (inverses, panels), (across, own)))
            ]
            for copy in copies:
                copy.start()
            copies[0].wait()
            packed[:half] = jnp.concatenate([here[:half], here[half:]], axis=1)
            copies[1].wait()

            def both(target):
                first = 2 * jnp.minimum(target, n_win - 1)
                return jnp.concatenate([panels[first], panels[first + 1]])

            for s, ref in enumerate(sent, 1):
                ref[...] = both(jnp.bitwise_xor(q, s))
            mine[...] = both(q)
            packed[half : half + pair] = mine[...]
            copies[2].wait()
            packed[half + pair :] = own[:units]

        packed, own, rhs, mine, *sent = call(
            prepare,
            [(half + pair + units, wide), (whole, rows), (rows, width)] + [(pair, wide)] * n_pair,
            [],
            first=[rhs, across, inverses],
            scratch=[pltpu.VMEM((n_pan, shard, wide), jnp.float32), pltpu.SemaphoreType.DMA((3,))],
        )

        beside = swap_rows(packed, lambda q: q < n_win)
        parts = [hop(sent[s - 1], lambda q, x, j, k, s=s: (q ^ s, k, j, x)) for s in range(1, n_pair)]
        own_along = along(own)

        def mix(*refs):
            parts, own, packed = refs[: n_pair - 1], refs[n_pair - 1 : -1], refs[-1]
            for s, ref in enumerate(parts):
                packed[s * pair : (s + 1) * pair] = ref[...]
            for s, ref in enumerate(own):
                packed[at_own + s * part : at_own + (s + 1) * part] = ref[:part]

        soon = call(mix, [(at_own + n_half * part, wide)], [*parts, own, *own_along], last=[beside])
        soon = [soon, swap_cores(soon)]

        def cut(beside, near):
            near[...] = beside[half + pair :]

        near = call(cut, [(units, rows)], [beside], last=parts)
        near = [near, *along(near, lambda q: 0 < q < n_win)]

        def rest(*refs):
            own, near, packed = refs[:n_half], refs[n_half:-1], refs[-1]
            for s, ref in enumerate(own):
                packed[s * far : (s + 1) * far] = ref[part:]
            for s, ref in enumerate(near):
                packed[n_half * far + s * units : n_half * far + (s + 1) * units] = ref[...]

        def columns(blocks, panel, count, row=0):
            got = []
            for p in range(panel, panel + count):
                for core in range(2):
                    for s in range(n_half):
                        if row:
                            ref, at = blocks[2 + core], n_half * far + s * units + p * part
                        elif p:
                            ref, at = blocks[2 + core], s * far + (p - 1) * part
                        else:
                            ref, at = blocks[core], at_own + s * part
                        got.append(ref[at : at + part])
            return jnp.concatenate(got)

        def assemble(soon, other, mine, beside, inverse):
            q, x, j, k = place()
            theirs = beside[half : half + pair]
            for m in range(2):
                at = m * shard
                got = [mine[at : at + shard], theirs[at : at + shard]]
                got = [jnp.where(x == 0, got[0], got[1]), jnp.where(x == 0, got[1], got[0])]
                for s in range(n_pair - 1):
                    a, b = (ref[s * pair + at : s * pair + at + shard] for ref in (soon, other))
                    got += [jnp.where(k == 0, a, b), jnp.where(k == 0, b, a)]
                inverse[m] = jnp.concatenate(got)

        def solve_first(soon, other, mine, beside, rhs, either, inverse, scratch):
            x = place()[1]

            @pl.when(place()[0] == 0)
            def _():
                assemble(soon, other, mine, beside, inverse)
                first = turn(dot(inverse[0], jnp.where(x == 0, rhs[...], unfold(beside))))
                scratch[...] = first
                either[...] = first

                @pl.when(x == 1)
                def _():
                    left = rhs[...] - dot(columns([soon, other], 0, 1), ordered(scratch), (0, 0))
                    either[...] = turn(dot(inverse[1], left))

        panel = pltpu.VMEM((rows, width), jnp.float32)
        inverse = pltpu.VMEM((2, wide, wide), jnp.float32)
        either = call(solve_first, [(rows, width)], [*soon, mine, beside, rhs], scratch=[inverse, panel])
        results = [either]

        def arrive(*refs, pairs):
            got = refs[0][...]
            for t, ref in zip(pairs[1:], refs[1:-1], strict=True):
                got = jnp.where(place()[0] == t, ref[...], got)
            refs[-1][...] = got

        early, blocks = [], None
        for w in range(n_win - 1):
            here = climb(either, w, w + 1)
            there = swap_rows(here, lambda q, w=w: q == w + 1)
            early.append([climb(here, w + 1, t) for t in range(n_pair - 1, w + 1, -1)])
            late = call(rest, [(n_half * (far + units), rows)], [own, *own_along, *near], last=[here])
            blocks = [*soon, late, swap_cores(late)]

            def lean(mine, beside, rhs, *refs):
                blocks, here, (fixed, slope, kept, inverse) = refs[:4], refs[4], refs[5:]
                x = place()[1]
                assemble(*blocks[:2], mine, beside, inverse)

                def solve(m, start, block, other):
                    fixed[...] = turn(dot(inverse[m], start))
                    slope[...] = turn(dot(inverse[m], block, (1, 1) if other else (1, 0)))

                mine = ordered(here)

                @pl.when(x == 0)
                def _():
                    start = rhs[...] - dot(columns(blocks, 0, 1), mine, (0, 0))
                    solve(0, start, columns(blocks, 1, 1), True)

                @pl.when(x == 1)
                def _():
                    start = unfold(beside) - dot(columns(blocks, 1, 1, 1), mine, (0, 0))
                    solve(0, start, columns(blocks, 0, 1, 1), True)
                    start = rhs[...] - dot(columns(blocks, 1, 1), mine, (0, 0))
                    step = columns(blocks, 2, 1)
                    start = start - dot(step, ordered(fixed), (0, 0))
                    kept[...] = slope[...]
                    block = columns(blocks, 0, 1).T - dot(step, ordered(kept), (0, 0))
                    solve(1, start, block, False)

            def solve_next(fixed, slope, there, either):
                either[...] = fixed[...] - dot(slope[...], ordered(there))

            fixed, slope = call(
                lean,
                [(rows, width), (rows, wide)],
                [mine, beside, rhs, *blocks, here],
                scratch=[pltpu.VMEM((rows, wide), jnp.float32), inverse],
            )
            either = call(solve_next, [(rows, width)], [fixed, slope, there])
            results.append(either)

        final = [climb(either, n_win - 1, t) for t in range(n_win, n_pair)]
        left = rhs
        for i, values in enumerate([*early, final]):
            pairs = range(n_win, n_pair) if i == len(early) else range(n_pair - 1, i + 1, -1)
            which = functools.partial(arrive, pairs=pairs)
            value = call(which, [(rows, width)], values, last=[either] if i < len(early) else [])
            traded = swap_rows(value, lambda q: q >= n_win)

            def update(start, *refs, other, at=2 * i):
                blocks, value, out = refs[:4], refs[4], refs[5]
                a, b = columns(blocks, at, 1), columns(blocks, at + 1, 1)
                block = jnp.where((place()[1] == 0) == other, b, a)
                out[...] = start[...] - dot(block, ordered(value), (0, 0))

            first = functools.partial(update, other=False)
            left = call(first, [(rows, width)], [left, *blocks, value])
            if i < len(early):
                left = call(functools.partial(update, other=True), [(rows, width)], [left, *blocks, traded])

        def finish(*refs):
            update(*refs[:6], refs[-1], other=True)
            for w in range(n_win):

                @pl.when(place()[0] == w)
                def _(w=w):
                    refs[-1][...] = refs[6 + w][...]

        return call(finish, [(rows, width)], [left, *blocks, traded, *results], home=True)

    placed = (P("row", "col"), P("row", None, "col"), P(None, "row", None))
    return jax.shard_map(body, mesh=mesh, in_specs=placed, out_specs=P("row", "col"), check_vma=False)
```

```python
import functools

import jax
import jax.numpy as jnp
from jax import lax
from jax.experimental import pallas as pl
from jax.experimental.pallas import tpu as pltpu
from jax.sharding import PartitionSpec as P

AXES = ("row", "col")
VMEM = pl.BlockSpec(memory_space=pltpu.VMEM)
ANY = pl.BlockSpec(memory_space=pl.ANY)
FREE = pl.CostEstimate(flops=0, bytes_accessed=0, transcendentals=0)
LIMIT = 24 * 1024 * 1024


def split(value):
    high = value.astype(jnp.bfloat16)
    return high, (value - high.astype(jnp.float32)).astype(jnp.bfloat16)


def dot(left, right, over=(1, 0)):
    (a, b), (c, d) = split(left), split(right)

    def one(u, v):
        return lax.dot_general(u, v, (((over[0],), (over[1],)), ((), ())), preferred_element_type=jnp.float32)

    return one(a, c) + (one(a, d) + one(b, c))


def call(body, shapes, held, first=(), last=(), home=False, scratch=()):
    out = [jax.ShapeDtypeStruct(s, jnp.float32) if home else pltpu.VMEM(s, jnp.float32) for s in shapes]
    n_in, n_last = len(first) + len(held), len(last)

    def kernel(*refs):
        body(*refs[:n_in], *refs[n_in + n_last :])

    got = pl.pallas_call(
        kernel,
        out_shape=out,
        in_specs=[ANY] * len(first) + [VMEM] * len(held) + [ANY] * n_last,
        out_specs=[VMEM] * len(shapes),
        scratch_shapes=scratch,
        cost_estimate=FREE,
        compiler_params=pltpu.CompilerParams(vmem_limit_bytes=LIMIT),
    )(
        *[pltpu.with_memory_space_constraint(v, pltpu.HBM) for v in first],
        *[pltpu.with_memory_space_constraint(v, pltpu.VMEM) for v in held],
        *last,
    )
    return got[0] if len(shapes) == 1 else got


def solution(mesh):
    n_row, n_col = mesh.shape["row"], mesh.shape["col"]
    n_pair, n_half = n_row // 2, n_col // 2

    def place():
        row, col = lax.axis_index("row"), lax.axis_index("col")
        return row // 2, row % 2, col // 2, col % 2

    def hop(value, move):
        edges = []
        for q in range(n_pair):
            for x in range(2):
                for j in range(n_half):
                    for k in range(2):
                        a, b, c, d = move(q, x, j, k) or (q, x, j, 1 - k)
                        edges.append(((q * 2 + x) * n_col + j * 2 + k, (a * 2 + b) * n_col + c * 2 + d))
        return lax.ppermute(value, AXES, edges)

    def every(q):
        return True

    def along(value, which=every):
        return [
            hop(value, lambda q, x, j, k, s=s: (q, x, (j + s) % n_half, k) if which(q) else None)
            for s in range(1, n_half)
        ]

    def swap_rows(value, which=every):
        return hop(value, lambda q, x, j, k: (q, 1 - x, j, k) if which(q) else None)

    def swap_cores(value):
        return hop(value, lambda q, x, j, k: None)

    def climb(value, w, t):
        return hop(value, lambda q, x, j, k: ({w: t, t: w}[q], x, j, k) if q in (w, t) else None)

    def body(rhs, factor, inverses):
        rows, n_pan, part = factor.shape
        width = rhs.shape[1]
        shard, wide = inverses.shape[1:]
        n_win = n_pan // 2
        half, pair, whole = rows // 2, 2 * shard, n_pan * part
        units = (n_pan - 2) * part
        at_own = (n_pair - 1) * pair
        far = whole - part

        def unfold(ref):
            return jnp.concatenate([ref[:half, :width], ref[:half, width:]])

        def ordered(ref):
            q, x, j, k = place()
            got = []
            for c in (k, 1 - k):
                for s in range(n_half):
                    start = pl.multiple_of((lax.rem(j - s + n_half, n_half) * 2 + c) * part, part)
                    got.append(ref[pl.ds(start, part), :])
            return jnp.concatenate(got)

        def turn(value):
            q, step = place()[0], 1
            while step < n_pair:
                run = step * pair
                pieces = [value[at : at + run] for at in range(0, n_pair * pair, run)]
                other = [pieces[i ^ 1] for i in range(len(pieces))]
                value = jnp.where((q // step) % 2 == 1, jnp.concatenate(other), value)
                step *= 2
            return value

        across = jnp.transpose(factor, (1, 2, 0)).reshape(-1, rows)

        def prepare(rhs, across, inverses, packed, own, here, mine, *refs):
            sent, panels, sems = refs[:-2], refs[-2], refs[-1]
            q = place()[0]
            copies = [
                pltpu.make_async_copy(a, b, sems.at[i])
                for i, (a, b) in enumerate(((rhs, here), (inverses, panels), (across, own)))
            ]
            for copy in copies:
                copy.start()
            copies[0].wait()
            packed[:half] = jnp.concatenate([here[:half], here[half:]], axis=1)
            copies[1].wait()

            def both(target):
                first = 2 * jnp.minimum(target, n_win - 1)
                return jnp.concatenate([panels[first], panels[first + 1]])

            for s, ref in enumerate(sent, 1):
                ref[...] = both(jnp.bitwise_xor(q, s))
            mine[...] = both(q)
            packed[half : half + pair] = mine[...]
            copies[2].wait()
            packed[half + pair :] = own[:units]

        packed, own, rhs, mine, *sent = call(
            prepare,
            [(half + pair + units, wide), (whole, rows), (rows, width)] + [(pair, wide)] * n_pair,
            [],
            first=[rhs, across, inverses],
            scratch=[pltpu.VMEM((n_pan, shard, wide), jnp.float32), pltpu.SemaphoreType.DMA((3,))],
        )

        beside = swap_rows(packed, lambda q: q < n_win)
        parts = [hop(sent[s - 1], lambda q, x, j, k, s=s: (q ^ s, k, j, x)) for s in range(1, n_pair)]
        own_along = along(own)

        def mix(*refs):
            parts, own, packed = refs[: n_pair - 1], refs[n_pair - 1 : -1], refs[-1]
            for s, ref in enumerate(parts):
                packed[s * pair : (s + 1) * pair] = ref[...]
            for s, ref in enumerate(own):
                packed[at_own + s * part : at_own + (s + 1) * part] = ref[:part]

        soon = call(mix, [(at_own + n_half * part, wide)], [*parts, own, *own_along], last=[beside])
        soon = [soon, swap_cores(soon)]

        def cut(beside, near):
            near[...] = beside[half + pair :]

        near = call(cut, [(units, rows)], [beside], last=parts)
        near = [near, *along(near, lambda q: 0 < q < n_win)]

        def rest(*refs):
            own, near, packed = refs[:n_half], refs[n_half], refs[-1]
            for s, ref in enumerate(own):
                packed[s * far : (s + 1) * far] = ref[part:]
            packed[n_half * far :] = near[...]

        more = call(rest, [(n_half * far + units, rows)], [own, *own_along, near[0]])
        more = [more, swap_cores(more)]

        def stack(*refs):
            for s, ref in enumerate(refs[:-1]):
                refs[-1][s * units : (s + 1) * units] = ref[...]

        def columns(blocks, panel, count, row=0):
            got = []
            for p in range(panel, panel + count):
                for core in range(2):
                    for s in range(n_half):
                        if row:
                            ref, at = blocks[2 + core], n_half * far + p * part
                            if s:
                                ref, at = blocks[4 + core], (s - 1) * units + p * part
                        elif p:
                            ref, at = blocks[2 + core], s * far + (p - 1) * part
                        else:
                            ref, at = blocks[core], at_own + s * part
                        got.append(ref[at : at + part])
            return jnp.concatenate(got)

        def assemble(soon, other, mine, beside, inverse):
            q, x, j, k = place()
            theirs = beside[half : half + pair]
            for m in range(2):
                at = m * shard
                got = [mine[at : at + shard], theirs[at : at + shard]]
                got = [jnp.where(x == 0, got[0], got[1]), jnp.where(x == 0, got[1], got[0])]
                for s in range(n_pair - 1):
                    a, b = (ref[s * pair + at : s * pair + at + shard] for ref in (soon, other))
                    got += [jnp.where(k == 0, a, b), jnp.where(k == 0, b, a)]
                inverse[m] = jnp.concatenate(got)

        def solve_first(soon, other, mine, beside, rhs, either, inverse, scratch):
            x = place()[1]

            @pl.when(place()[0] == 0)
            def _():
                assemble(soon, other, mine, beside, inverse)
                first = turn(dot(inverse[0], jnp.where(x == 0, rhs[...], unfold(beside))))
                scratch[...] = first
                either[...] = first

                @pl.when(x == 1)
                def _():
                    left = rhs[...] - dot(columns([soon, other], 0, 1), ordered(scratch), (0, 0))
                    either[...] = turn(dot(inverse[1], left))

        panel = pltpu.VMEM((rows, width), jnp.float32)
        inverse = pltpu.VMEM((2, wide, wide), jnp.float32)
        either = call(solve_first, [(rows, width)], [*soon, mine, beside, rhs], scratch=[inverse, panel])
        results = [either]

        def arrive(*refs, pairs):
            got = refs[0][:rows]
            for t, ref in zip(pairs[1:], refs[1:-1], strict=True):
                got = jnp.where(place()[0] == t, ref[:rows], got)
            refs[-1][...] = got

        early, blocks = [], None
        for w in range(n_win - 1):
            here = climb(either, w, w + 1)
            there = swap_rows(here, lambda q, w=w: q == w + 1)
            early.append([climb(here, w + 1, t) for t in range(n_pair - 1, w + 1, -1)])
            late = call(stack, [((n_half - 1) * units, rows)], near[1:], last=[either])
            blocks = [*soon, *more, late, swap_cores(late)]

            def lean(mine, beside, rhs, *refs):
                blocks, here, (fixed, slope, kept, inverse) = refs[:6], refs[6], refs[7:]
                x = place()[1]
                assemble(*blocks[:2], mine, beside, inverse)

                def solve(m, start, block, other):
                    fixed[...] = turn(dot(inverse[m], start))
                    slope[...] = turn(dot(inverse[m], block, (1, 1) if other else (1, 0)))

                mine = ordered(here)

                @pl.when(x == 0)
                def _():
                    start = rhs[...] - dot(columns(blocks, 0, 1), mine, (0, 0))
                    solve(0, start, columns(blocks, 1, 1), True)

                @pl.when(x == 1)
                def _():
                    start = unfold(beside) - dot(columns(blocks, 1, 1, 1), mine, (0, 0))
                    solve(0, start, columns(blocks, 0, 1, 1), True)
                    start = rhs[...] - dot(columns(blocks, 1, 1), mine, (0, 0))
                    step = columns(blocks, 2, 1)
                    start = start - dot(step, ordered(fixed), (0, 0))
                    kept[...] = slope[...]
                    block = columns(blocks, 0, 1).T - dot(step, ordered(kept), (0, 0))
                    solve(1, start, block, False)

            def solve_next(fixed, slope, there, either):
                either[...] = fixed[...] - dot(slope[...], ordered(there))

            fixed, slope = call(
                lean,
                [(rows, width), (rows, wide)],
                [mine, beside, rhs, *blocks, here],
                scratch=[pltpu.VMEM((rows, wide), jnp.float32), inverse],
            )
            either = call(solve_next, [(rows, width)], [fixed, slope, there])
            results.append(either)

        final = [climb(either, n_win - 1, t) for t in range(n_win, n_pair)]
        left = rhs
        for i, values in enumerate([*early, final]):
            pairs = range(n_win, n_pair) if i == len(early) else range(n_pair - 1, i + 1, -1)
            which = functools.partial(arrive, pairs=pairs)
            value = call(which, [(rows, width)], values, last=[either] if i < len(early) else [])
            traded = swap_rows(value, lambda q: q >= n_win)

            def update(start, *refs, other, at=2 * i):
                blocks, value, out = refs[:6], refs[6], refs[7]
                a, b = columns(blocks, at, 1), columns(blocks, at + 1, 1)
                block = jnp.where((place()[1] == 0) == other, b, a)
                out[...] = start[...] - dot(block, ordered(value), (0, 0))

            first = functools.partial(update, other=False)
            left = call(first, [(rows, width)], [left, *blocks, value])
            if i < len(early):
                left = call(functools.partial(update, other=True), [(rows, width)], [left, *blocks, traded])

        def finish(*refs):
            update(*refs[:8], refs[-1], other=True)
            for w in range(n_win):

                @pl.when(place()[0] == w)
                def _(w=w):
                    refs[-1][...] = refs[8 + w][...]

        return call(finish, [(rows, width)], [left, *blocks, traded, *results], home=True)

    placed = (P("row", "col"), P("row", None, "col"), P(None, "row", None))
    return jax.shard_map(body, mesh=mesh, in_specs=placed, out_specs=P("row", "col"), check_vma=False)
```

```python
import functools

import jax
import jax.numpy as jnp
from jax import lax
from jax.experimental import pallas as pl
from jax.experimental.pallas import tpu as pltpu
from jax.sharding import PartitionSpec as P

AXES = ("row", "col")
VMEM = pl.BlockSpec(memory_space=pltpu.VMEM)
ANY = pl.BlockSpec(memory_space=pl.ANY)
FREE = pl.CostEstimate(flops=0, bytes_accessed=0, transcendentals=0)
LIMIT = 24 * 1024 * 1024


def split(value):
    high = value.astype(jnp.bfloat16)
    return high, (value - high.astype(jnp.float32)).astype(jnp.bfloat16)


def dot(left, right, over=(1, 0)):
    (a, b), (c, d) = split(left), split(right)

    def one(u, v):
        return lax.dot_general(u, v, (((over[0],), (over[1],)), ((), ())), preferred_element_type=jnp.float32)

    return one(a, c) + (one(a, d) + one(b, c))


def call(body, shapes, held, first=(), last=(), home=False, scratch=()):
    out = [jax.ShapeDtypeStruct(s, jnp.float32) if home else pltpu.VMEM(s, jnp.float32) for s in shapes]
    n_in, n_last = len(first) + len(held), len(last)

    def kernel(*refs):
        body(*refs[:n_in], *refs[n_in + n_last :])

    got = pl.pallas_call(
        kernel,
        out_shape=out,
        in_specs=[ANY] * len(first) + [VMEM] * len(held) + [ANY] * n_last,
        out_specs=[VMEM] * len(shapes),
        scratch_shapes=scratch,
        cost_estimate=FREE,
        compiler_params=pltpu.CompilerParams(vmem_limit_bytes=LIMIT),
    )(
        *[pltpu.with_memory_space_constraint(v, pltpu.HBM) for v in first],
        *[pltpu.with_memory_space_constraint(v, pltpu.VMEM) for v in held],
        *last,
    )
    return got[0] if len(shapes) == 1 else got


def solution(mesh):
    n_row, n_col = mesh.shape["row"], mesh.shape["col"]
    n_pair, n_half = n_row // 2, n_col // 2

    def place():
        row, col = lax.axis_index("row"), lax.axis_index("col")
        return row // 2, row % 2, col // 2, col % 2

    def hop(value, move):
        edges = []
        for q in range(n_pair):
            for x in range(2):
                for j in range(n_half):
                    for k in range(2):
                        a, b, c, d = move(q, x, j, k) or (q, x, j, 1 - k)
                        edges.append(((q * 2 + x) * n_col + j * 2 + k, (a * 2 + b) * n_col + c * 2 + d))
        return lax.ppermute(value, AXES, edges)

    def every(q):
        return True

    def along(value, which=every):
        return [
            hop(value, lambda q, x, j, k, s=s: (q, x, (j + s) % n_half, k) if which(q) else None)
            for s in range(1, n_half)
        ]

    def swap_rows(value, which=every):
        return hop(value, lambda q, x, j, k: (q, 1 - x, j, k) if which(q) else None)

    def swap_cores(value):
        return hop(value, lambda q, x, j, k: None)

    def climb(value, w, t):
        return hop(value, lambda q, x, j, k: ({w: t, t: w}[q], x, j, k) if q in (w, t) else None)

    def body(rhs, factor, inverses):
        rows, n_pan, part = factor.shape
        width = rhs.shape[1]
        shard, wide = inverses.shape[1:]
        n_win = n_pan // 2
        half, pair, whole = rows // 2, 2 * shard, n_pan * part
        units = (n_pan - 2) * part
        at_own = (n_pair - 1) * pair
        far = whole - part

        def unfold(ref):
            return jnp.concatenate([ref[:half, :width], ref[:half, width:]])

        def ordered(ref):
            q, x, j, k = place()
            got = []
            for c in (k, 1 - k):
                for s in range(n_half):
                    start = pl.multiple_of((lax.rem(j - s + n_half, n_half) * 2 + c) * part, part)
                    got.append(ref[pl.ds(start, part), :])
            return jnp.concatenate(got)

        def turn(value):
            q, step = place()[0], 1
            while step < n_pair:
                run = step * pair
                pieces = [value[at : at + run] for at in range(0, n_pair * pair, run)]
                other = [pieces[i ^ 1] for i in range(len(pieces))]
                value = jnp.where((q // step) % 2 == 1, jnp.concatenate(other), value)
                step *= 2
            return value

        across = jnp.transpose(factor, (1, 2, 0)).reshape(-1, rows)

        def prepare(rhs, across, inverses, packed, own, here, mine, *refs):
            sent, panels, sems = refs[:-2], refs[-2], refs[-1]
            q = place()[0]
            copies = [
                pltpu.make_async_copy(a, b, sems.at[i])
                for i, (a, b) in enumerate(((rhs, here), (inverses, panels), (across, own)))
            ]
            for copy in copies:
                copy.start()
            copies[0].wait()
            packed[:half] = jnp.concatenate([here[:half], here[half:]], axis=1)
            copies[1].wait()

            def both(target):
                first = 2 * jnp.minimum(target, n_win - 1)
                return jnp.concatenate([panels[first], panels[first + 1]])

            for s, ref in enumerate(sent, 1):
                ref[...] = both(jnp.bitwise_xor(q, s))
            mine[...] = both(q)
            packed[half : half + pair] = mine[...]
            copies[2].wait()
            packed[half + pair :] = own[:units]

        packed, own, rhs, mine, *sent = call(
            prepare,
            [(half + pair + units, wide), (whole, rows), (rows, width)] + [(pair, wide)] * n_pair,
            [],
            first=[rhs, across, inverses],
            scratch=[pltpu.VMEM((n_pan, shard, wide), jnp.float32), pltpu.SemaphoreType.DMA((3,))],
        )

        beside = swap_rows(packed, lambda q: q < n_win)
        parts = [hop(sent[s - 1], lambda q, x, j, k, s=s: (q ^ s, k, j, x)) for s in range(1, n_pair)]
        own_along = along(own)

        def mix(*refs):
            parts, own, packed = refs[: n_pair - 1], refs[n_pair - 1 : -1], refs[-1]
            for s, ref in enumerate(parts):
                packed[s * pair : (s + 1) * pair] = ref[...]
            for s, ref in enumerate(own):
                packed[at_own + s * part : at_own + (s + 1) * part] = ref[:part]

        soon = call(mix, [(at_own + n_half * part, wide)], [*parts, own, *own_along], last=[beside])
        soon = [soon, swap_cores(soon)]

        def cut(beside, near):
            near[...] = beside[half + pair :]

        near = call(cut, [(units, rows)], [beside], last=parts)
        near = [near, *along(near, lambda q: 0 < q < n_win)]

        def rest(*refs):
            own, near, packed = refs[:n_half], refs[n_half], refs[-1]
            for s, ref in enumerate(own):
                packed[s * far : (s + 1) * far] = ref[part:]
            packed[n_half * far :] = near[...]

        more = call(rest, [(n_half * far + units, rows)], [own, *own_along, near[0]])
        more = [more, swap_cores(more)]

        def stack(*refs):
            for s, ref in enumerate(refs[:-1]):
                refs[-1][s * units : (s + 1) * units] = ref[...]

        def columns(blocks, panel, count, row=0):
            got = []
            for p in range(panel, panel + count):
                for core in range(2):
                    for s in range(n_half):
                        if row:
                            ref, at = blocks[2 + core], n_half * far + p * part
                            if s:
                                ref, at = blocks[4 + core], (s - 1) * units + p * part
                        elif p:
                            ref, at = blocks[2 + core], s * far + (p - 1) * part
                        else:
                            ref, at = blocks[core], at_own + s * part
                        got.append(ref[at : at + part])
            return jnp.concatenate(got)

        def assemble(soon, other, mine, beside, inverse):
            q, x, j, k = place()
            theirs = beside[half : half + pair]
            for m in range(2):
                at = m * shard
                got = [mine[at : at + shard], theirs[at : at + shard]]
                got = [jnp.where(x == 0, got[0], got[1]), jnp.where(x == 0, got[1], got[0])]
                for s in range(n_pair - 1):
                    a, b = (ref[s * pair + at : s * pair + at + shard] for ref in (soon, other))
                    got += [jnp.where(k == 0, a, b), jnp.where(k == 0, b, a)]
                inverse[m] = jnp.concatenate(got)

        def solve_first(soon, other, mine, beside, rhs, either, inverse, scratch):
            x = place()[1]

            @pl.when(place()[0] == 0)
            def _():
                assemble(soon, other, mine, beside, inverse)
                first = turn(dot(inverse[0], jnp.where(x == 0, rhs[...], unfold(beside))))
                scratch[...] = first
                either[...] = first

                @pl.when(x == 1)
                def _():
                    left = rhs[...] - dot(columns([soon, other], 0, 1), ordered(scratch), (0, 0))
                    either[...] = turn(dot(inverse[1], left))

        panel = pltpu.VMEM((rows, width), jnp.float32)
        inverse = pltpu.VMEM((2, wide, wide), jnp.float32)
        either = call(solve_first, [(rows, width)], [*soon, mine, beside, rhs], scratch=[inverse, panel])
        results = [either]

        def arrive(*refs, pairs):
            got = refs[0][:rows]
            for t, ref in zip(pairs[1:], refs[1:-1], strict=True):
                got = jnp.where(place()[0] == t, ref[:rows], got)
            refs[-1][...] = got

        early, blocks = [], None
        for w in range(n_win - 1):
            here = climb(either, w, w + 1)
            there = swap_rows(here, lambda q, w=w: q == w + 1)
            early.append([climb(here, w + 1, t) for t in range(n_pair - 1, w + 1, -1)])
            late = call(stack, [((n_half - 1) * units, rows)], near[1:], last=[either])
            blocks = [*soon, *more, late, swap_cores(late)]

            def lean(mine, beside, rhs, *refs, w=w):
                blocks, here, (fixed, slope, kept, inverse) = refs[:6], refs[6], refs[7:]
                x = place()[1]
                here_too = place()[0] == w + 1

                @pl.when(here_too)
                def _():
                    assemble(*blocks[:2], mine, beside, inverse)

                def solve(m, start, block, other):
                    fixed[...] = turn(dot(inverse[m], start))
                    slope[...] = turn(dot(inverse[m], block, (1, 1) if other else (1, 0)))

                mine = ordered(here)

                @pl.when(jnp.logical_and(here_too, x == 0))
                def _():
                    start = rhs[...] - dot(columns(blocks, 0, 1), mine, (0, 0))
                    solve(0, start, columns(blocks, 1, 1), True)

                @pl.when(jnp.logical_and(here_too, x == 1))
                def _():
                    start = unfold(beside) - dot(columns(blocks, 1, 1, 1), mine, (0, 0))
                    solve(0, start, columns(blocks, 0, 1, 1), True)
                    start = rhs[...] - dot(columns(blocks, 1, 1), mine, (0, 0))
                    step = columns(blocks, 2, 1)
                    start = start - dot(step, ordered(fixed), (0, 0))
                    kept[...] = slope[...]
                    block = columns(blocks, 0, 1).T - dot(step, ordered(kept), (0, 0))
                    solve(1, start, block, False)

            def solve_next(fixed, slope, there, either):
                either[...] = fixed[...] - dot(slope[...], ordered(there))

            fixed, slope = call(
                lean,
                [(rows, width), (rows, wide)],
                [mine, beside, rhs, *blocks, here],
                scratch=[pltpu.VMEM((rows, wide), jnp.float32), inverse],
            )
            either = call(solve_next, [(rows, width)], [fixed, slope, there])
            results.append(either)

        final = [climb(either, n_win - 1, t) for t in range(n_win, n_pair)]
        left = rhs
        for i, values in enumerate([*early, final]):
            pairs = range(n_win, n_pair) if i == len(early) else range(n_pair - 1, i + 1, -1)
            which = functools.partial(arrive, pairs=pairs)
            value = call(which, [(rows, width)], values, last=[either] if i < len(early) else [])
            traded = swap_rows(value, lambda q: q >= n_win)

            def update(start, *refs, other, at=2 * i):
                blocks, value, out = refs[:6], refs[6], refs[7]
                a, b = columns(blocks, at, 1), columns(blocks, at + 1, 1)
                block = jnp.where((place()[1] == 0) == other, b, a)
                out[...] = start[...] - dot(block, ordered(value), (0, 0))

            first = functools.partial(update, other=False)
            left = call(first, [(rows, width)], [left, *blocks, value])
            if i < len(early):
                left = call(functools.partial(update, other=True), [(rows, width)], [left, *blocks, traded])

        def finish(*refs):
            update(*refs[:8], refs[-1], other=True)
            for w in range(n_win):

                @pl.when(place()[0] == w)
                def _(w=w):
                    refs[-1][...] = refs[8 + w][...]

        return call(finish, [(rows, width)], [left, *blocks, traded, *results], home=True)

    placed = (P("row", "col"), P("row", None, "col"), P(None, "row", None))
    return jax.shard_map(body, mesh=mesh, in_specs=placed, out_specs=P("row", "col"), check_vma=False)
```

```python
import functools

import jax
import jax.numpy as jnp
from jax import lax
from jax.experimental import pallas as pl
from jax.experimental.pallas import tpu as pltpu
from jax.sharding import PartitionSpec as P

AXES = ("row", "col")
VMEM = pl.BlockSpec(memory_space=pltpu.VMEM)
ANY = pl.BlockSpec(memory_space=pl.ANY)
FREE = pl.CostEstimate(flops=0, bytes_accessed=0, transcendentals=0)
LIMIT = 24 * 1024 * 1024


def split(value):
    high = value.astype(jnp.bfloat16)
    return high, (value - high.astype(jnp.float32)).astype(jnp.bfloat16)


def dot(left, right, over=(1, 0)):
    (a, b), (c, d) = split(left), split(right)

    def one(u, v):
        return lax.dot_general(u, v, (((over[0],), (over[1],)), ((), ())), preferred_element_type=jnp.float32)

    return one(a, c) + (one(a, d) + one(b, c))


def call(body, shapes, held, first=(), last=(), home=False, scratch=()):
    out = [jax.ShapeDtypeStruct(s, jnp.float32) if home else pltpu.VMEM(s, jnp.float32) for s in shapes]
    n_in, n_last = len(first) + len(held), len(last)

    def kernel(*refs):
        body(*refs[:n_in], *refs[n_in + n_last :])

    got = pl.pallas_call(
        kernel,
        out_shape=out,
        in_specs=[ANY] * len(first) + [VMEM] * len(held) + [ANY] * n_last,
        out_specs=[VMEM] * len(shapes),
        scratch_shapes=scratch,
        cost_estimate=FREE,
        compiler_params=pltpu.CompilerParams(vmem_limit_bytes=LIMIT),
    )(
        *[pltpu.with_memory_space_constraint(v, pltpu.HBM) for v in first],
        *[pltpu.with_memory_space_constraint(v, pltpu.VMEM) for v in held],
        *last,
    )
    return got[0] if len(shapes) == 1 else got


def solution(mesh):
    n_row, n_col = mesh.shape["row"], mesh.shape["col"]
    n_pair, n_half = n_row // 2, n_col // 2

    def place():
        row, col = lax.axis_index("row"), lax.axis_index("col")
        return row // 2, row % 2, col // 2, col % 2

    def hop(value, move):
        edges = []
        for q in range(n_pair):
            for x in range(2):
                for j in range(n_half):
                    for k in range(2):
                        a, b, c, d = move(q, x, j, k) or (q, x, j, 1 - k)
                        edges.append(((q * 2 + x) * n_col + j * 2 + k, (a * 2 + b) * n_col + c * 2 + d))
        return lax.ppermute(value, AXES, edges)

    def every(q):
        return True

    def along(value, which=every):
        return [
            hop(value, lambda q, x, j, k, s=s: (q, x, (j + s) % n_half, k) if which(q) else None)
            for s in range(1, n_half)
        ]

    def swap_rows(value, which=every):
        return hop(value, lambda q, x, j, k: (q, 1 - x, j, k) if which(q) else None)

    def swap_cores(value):
        return hop(value, lambda q, x, j, k: None)

    def climb(value, w, t):
        return hop(value, lambda q, x, j, k: ({w: t, t: w}[q], x, j, k) if q in (w, t) else None)

    def body(rhs, factor, inverses):
        rows, n_pan, part = factor.shape
        width = rhs.shape[1]
        shard, wide = inverses.shape[1:]
        n_win = n_pan // 2
        half, pair, whole = rows // 2, 2 * shard, n_pan * part
        units = (n_pan - 2) * part
        at_own = (n_pair - 1) * pair
        far = whole - part

        def unfold(ref):
            return jnp.concatenate([ref[:half, :width], ref[:half, width:]])

        def ordered(ref):
            q, x, j, k = place()
            got = []
            for c in (k, 1 - k):
                for s in range(n_half):
                    start = pl.multiple_of((lax.rem(j - s + n_half, n_half) * 2 + c) * part, part)
                    got.append(ref[pl.ds(start, part), :])
            return jnp.concatenate(got)

        def turn(value):
            q, step = place()[0], 1
            while step < n_pair:
                run = step * pair
                pieces = [value[at : at + run] for at in range(0, n_pair * pair, run)]
                other = [pieces[i ^ 1] for i in range(len(pieces))]
                value = jnp.where((q // step) % 2 == 1, jnp.concatenate(other), value)
                step *= 2
            return value

        across = jnp.transpose(factor, (1, 2, 0)).reshape(-1, rows)

        def prepare(rhs, across, inverses, packed, own, here, mine, *refs):
            sent, panels, sems = refs[:-2], refs[-2], refs[-1]
            q = place()[0]
            copies = [
                pltpu.make_async_copy(a, b, sems.at[i])
                for i, (a, b) in enumerate(((rhs, here), (inverses, panels), (across, own)))
            ]
            for copy in copies:
                copy.start()
            copies[0].wait()
            packed[:half] = jnp.concatenate([here[:half], here[half:]], axis=1)
            copies[1].wait()

            def both(target):
                first = 2 * jnp.minimum(target, n_win - 1)
                return jnp.concatenate([panels[first], panels[first + 1]])

            for s, ref in enumerate(sent, 1):
                ref[...] = both(jnp.bitwise_xor(q, s))
            mine[...] = both(q)
            packed[half : half + pair] = mine[...]
            copies[2].wait()
            packed[half + pair :] = own[:units]

        packed, own, rhs, mine, *sent = call(
            prepare,
            [(half + pair + units, wide), (whole, rows), (rows, width)] + [(pair, wide)] * n_pair,
            [],
            first=[rhs, across, inverses],
            scratch=[pltpu.VMEM((n_pan, shard, wide), jnp.float32), pltpu.SemaphoreType.DMA((3,))],
        )

        beside = swap_rows(packed, lambda q: q < n_win)
        parts = [hop(sent[s - 1], lambda q, x, j, k, s=s: (q ^ s, k, j, x)) for s in range(1, n_pair)]
        own_along = along(own)

        def mix(*refs):
            parts, own, packed = refs[: n_pair - 1], refs[n_pair - 1 : -1], refs[-1]
            for s, ref in enumerate(parts):
                packed[s * pair : (s + 1) * pair] = ref[...]
            for s, ref in enumerate(own):
                packed[at_own + s * part : at_own + (s + 1) * part] = ref[:part]

        soon = call(mix, [(at_own + n_half * part, wide)], [*parts, own, *own_along], last=[beside])
        soon = [soon, swap_cores(soon)]

        def cut(beside, near):
            near[...] = beside[half + pair :]

        near = call(cut, [(units, rows)], [beside], last=parts)
        near = [near, *along(near, lambda q: 0 < q < n_win)]

        def rest(*refs):
            own, near, packed = refs[:n_half], refs[n_half], refs[-1]
            for s, ref in enumerate(own):
                packed[s * far : (s + 1) * far] = ref[part:]
            packed[n_half * far :] = near[...]

        more = call(rest, [(n_half * far + units, rows)], [own, *own_along, near[0]])
        more = [more, swap_cores(more)]

        def stack(*refs):
            for s, ref in enumerate(refs[:-1]):
                refs[-1][s * units : (s + 1) * units] = ref[...]

        def columns(blocks, panel, count, row=0):
            got = []
            for p in range(panel, panel + count):
                for core in range(2):
                    for s in range(n_half):
                        if row:
                            ref, at = blocks[2 + core], n_half * far + p * part
                            if s:
                                ref, at = blocks[4 + core], (s - 1) * units + p * part
                        elif p:
                            ref, at = blocks[2 + core], s * far + (p - 1) * part
                        else:
                            ref, at = blocks[core], at_own + s * part
                        got.append(ref[at : at + part])
            return jnp.concatenate(got)

        def assemble(soon, other, mine, beside, inverse):
            q, x, j, k = place()
            theirs = beside[half : half + pair]
            for m in range(2):
                at = m * shard
                got = [mine[at : at + shard], theirs[at : at + shard]]
                got = [jnp.where(x == 0, got[0], got[1]), jnp.where(x == 0, got[1], got[0])]
                for s in range(n_pair - 1):
                    a, b = (ref[s * pair + at : s * pair + at + shard] for ref in (soon, other))
                    got += [jnp.where(k == 0, a, b), jnp.where(k == 0, b, a)]
                inverse[m] = jnp.concatenate(got)

        def solve_first(soon, other, mine, beside, rhs, either, inverse, scratch):
            x = place()[1]

            @pl.when(place()[0] == 0)
            def _():
                assemble(soon, other, mine, beside, inverse)
                first = turn(dot(inverse[0], jnp.where(x == 0, rhs[...], unfold(beside))))
                scratch[...] = first
                either[...] = first

                @pl.when(x == 1)
                def _():
                    left = rhs[...] - dot(columns([soon, other], 0, 1), ordered(scratch), (0, 0))
                    either[...] = turn(dot(inverse[1], left))

        panel = pltpu.VMEM((rows, width), jnp.float32)
        inverse = pltpu.VMEM((2, wide, wide), jnp.float32)
        either = call(solve_first, [(rows, width)], [*soon, mine, beside, rhs], scratch=[inverse, panel])
        results = [either]

        def arrive(*refs, pairs):
            got = refs[0][:rows]
            for t, ref in zip(pairs[1:], refs[1:-1], strict=True):
                got = jnp.where(place()[0] == t, ref[:rows], got)
            refs[-1][...] = got

        early, blocks = [], None
        for w in range(n_win - 1):
            here = climb(either, w, w + 1)
            there = swap_rows(here, lambda q, w=w: q == w + 1)
            early.append([climb(here, w + 1, t) for t in range(w + 2, n_pair)])
            late = call(stack, [((n_half - 1) * units, rows)], near[1:], last=[either])
            blocks = [*soon, *more, late, swap_cores(late)]

            def lean(mine, beside, rhs, *refs, w=w):
                blocks, here, (fixed, slope, kept, inverse) = refs[:6], refs[6], refs[7:]
                x = place()[1]
                here_too = place()[0] == w + 1

                @pl.when(here_too)
                def _():
                    assemble(*blocks[:2], mine, beside, inverse)

                def solve(m, start, block, other):
                    fixed[...] = turn(dot(inverse[m], start))
                    slope[...] = turn(dot(inverse[m], block, (1, 1) if other else (1, 0)))

                mine = ordered(here)

                @pl.when(jnp.logical_and(here_too, x == 0))
                def _():
                    start = rhs[...] - dot(columns(blocks, 0, 1), mine, (0, 0))
                    solve(0, start, columns(blocks, 1, 1), True)

                @pl.when(jnp.logical_and(here_too, x == 1))
                def _():
                    start = unfold(beside) - dot(columns(blocks, 1, 1, 1), mine, (0, 0))
                    solve(0, start, columns(blocks, 0, 1, 1), True)
                    start = rhs[...] - dot(columns(blocks, 1, 1), mine, (0, 0))
                    step = columns(blocks, 2, 1)
                    start = start - dot(step, ordered(fixed), (0, 0))
                    kept[...] = slope[...]
                    block = columns(blocks, 0, 1).T - dot(step, ordered(kept), (0, 0))
                    solve(1, start, block, False)

            def solve_next(fixed, slope, there, either):
                either[...] = fixed[...] - dot(slope[...], ordered(there))

            fixed, slope = call(
                lean,
                [(rows, width), (rows, wide)],
                [mine, beside, rhs, *blocks, here],
                scratch=[pltpu.VMEM((rows, wide), jnp.float32), inverse],
            )
            either = call(solve_next, [(rows, width)], [fixed, slope, there])
            results.append(either)

        final = [climb(either, n_win - 1, t) for t in range(n_win, n_pair)]
        left = rhs
        for i, values in enumerate([*early, final]):
            pairs = range(n_win, n_pair) if i == len(early) else range(i + 2, n_pair)
            which = functools.partial(arrive, pairs=pairs)
            value = call(which, [(rows, width)], values, last=[either] if i < len(early) else [])
            traded = swap_rows(value, lambda q: q >= n_win)

            def update(start, *refs, other, at=2 * i):
                blocks, value, out = refs[:6], refs[6], refs[7]
                a, b = columns(blocks, at, 1), columns(blocks, at + 1, 1)
                block = jnp.where((place()[1] == 0) == other, b, a)
                out[...] = start[...] - dot(block, ordered(value), (0, 0))

            first = functools.partial(update, other=False)
            left = call(first, [(rows, width)], [left, *blocks, value])
            if i < len(early):
                left = call(functools.partial(update, other=True), [(rows, width)], [left, *blocks, traded])

        def finish(*refs):
            update(*refs[:8], refs[-1], other=True)
            for w in range(n_win):

                @pl.when(place()[0] == w)
                def _(w=w):
                    refs[-1][...] = refs[8 + w][...]

        return call(finish, [(rows, width)], [left, *blocks, traded, *results], home=True)

    placed = (P("row", "col"), P("row", None, "col"), P(None, "row", None))
    return jax.shard_map(body, mesh=mesh, in_specs=placed, out_specs=P("row", "col"), check_vma=False)
```
